1024 devices in a mesh: dp: 16 (over z, core), blk: 16 (over y_lo, x), pack: 4 (over y_hi).
Axes of the slice: x: 8, y: 8 (y_hi: 4, y_lo: 2; y = y_hi * 2 + y_lo), z: 8, core: 2. Of those that a mesh axis runs over, the one named last changes fastest.
Arguments:
- points: bfloat16 [1572864, 256], P(('dp', 'blk', 'pack')), may hold values from -6 to 6
- neighbours: int32 [27, 1572864], P(None, ('dp', 'blk', 'pack')), may hold values from 0 to 127, as said below
- tile_points: int32 [12288], P(('dp', 'blk', 'pack')), may hold values from 1 to 128
- tile_shape: int32 [12288], P(('dp', 'blk', 'pack')), may hold values from 0 to 6143, as said below
- captions: bfloat16 [6144, 1280], P(('dp', 'blk', 'pack')), may hold values from -6 to 6
- positive: int32 [6144], P(('dp', 'blk', 'pack')), may hold values from 0 to 95
- self_weight: bfloat16 [256, 256], replicated, may hold values from -0.375 to 0.375
- neighbour_weight: bfloat16 [256, 256], replicated, may hold values from -0.375 to 0.375
- projection: bfloat16 [256, 1280], replicated, may hold values from -0.375 to 0.375
- logit_scale: float32 [1], replicated, may hold values from 3 to 10
- logit_bias: float32 [1], replicated, may hold values from -4 to -1
Outputs:
- caption_grad: float32 [6144, 1280], P(('dp', 'blk', 'pack'))
- projection_grad: float32 [256, 1280], P('dp')
The draws below stay inside these ranges and needn't reach their ends.
Inputs may be any that keep to these rules, and one draw needn't show every extreme that they name: `neighbours`: every entry of a point is below the tile_points of that point's tile. A tile's shape belongs to a device of the tile's own pack group: tile_shape // 6 // 4 equals the holding device's number // 4. Each device holds exactly one tile of each of its own 6 shapes, and at most 6 tiles of the shapes of any one other device. Every shape has a tile.
All inputs are finite; a program needn't handle non-finite values.
Results may differ from the reference program's by a relative error of at most 0.0044.
Values may be sent and summed in bfloat16 or wider, within the bound.
No kernel may reach another device: no remote copies, remote signals or barrier semaphores. Data moves between devices by JAX's collectives and lax.ppermute only.
A program may use at most 32 MiB of HBM per device.

```python
import math
import jax
import jax.numpy as jnp
from jax import lax

CH = 256
EMB = 1280
NEIGH = 27
TILE_PTS = 128
TILES = 12
CAP = 6
S_DEV = 6
T_ALL = 12288
S_ALL = 6144
N_DP = 16
N_BLK = 16
N_PACK = 4


def shared_points(key):
    sub_key = jax.random.fold_in(key, 11)
    values = jax.random.randint(sub_key, (T_ALL,), 1, 2 * TILE_PTS)
    return jnp.minimum(values, TILE_PTS).astype(jnp.int32)


def draw_tile_points(key, part):
    counts = shared_points(key)
    return counts


def draw_neighbours(key, part):
    counts = shared_points(key)
    key = jax.random.fold_in(key, 2)
    raw_values = jax.random.randint(key, (NEIGH, T_ALL * TILE_PTS), 0, 1048576)
    limit = jnp.repeat(counts, TILE_PTS)
    return (raw_values % limit[None, :]).astype(jnp.int32)


def draw_tile_shape(key, part):
    key = jax.random.fold_in(key, 3)
    groups = T_ALL // (N_PACK * TILES)
    others = TILES - CAP
    keys = jax.random.split(key, 9)
    shape_other = (groups, N_PACK, others)
    preference = jnp.minimum(jax.random.randint(keys[0], shape_other, 0, N_PACK), jax.random.randint(keys[1], shape_other, 0, N_PACK))
    preference = jnp.minimum(preference, jax.random.randint(keys[2], shape_other, 0, N_PACK))
    ordering = jax.vmap(lambda subkey: jax.random.permutation(subkey, N_PACK))(jax.random.split(keys[3], groups)).astype(jnp.int32)
    owner_index = jnp.arange(N_PACK, dtype=jnp.int32)
    target = jnp.sum(ordering[:, None, None, :] * (preference[..., None] == owner_index).astype(jnp.int32), axis=-1)
    sender = owner_index[None, :, None]
    detour = (sender + 1 + jax.random.randint(keys[4], shape_other, 0, N_PACK - 1)) % N_PACK
    target = jnp.where(target == sender, detour, target)
    offset = jax.random.randint(keys[5], (groups, N_PACK, 1), 0, S_DEV)
    other_slot = jnp.minimum(jax.random.randint(keys[6], shape_other, 0, S_DEV), jax.random.randint(keys[7], shape_other, 0, S_DEV))
    other_slot = (other_slot + offset) % S_DEV
    own_owner = jnp.broadcast_to(sender, (groups, N_PACK, CAP))
    own_slot = jnp.broadcast_to(jnp.arange(CAP, dtype=jnp.int32)[None, None, :], (groups, N_PACK, CAP))
    owners = jnp.concatenate([own_owner, target], axis=2)
    slots = jnp.concatenate([own_slot, other_slot], axis=2)
    group_index = jnp.arange(groups, dtype=jnp.int32)[:, None, None]
    shape_ids = (group_index * N_PACK + owners) * S_DEV + slots
    shuffle = jax.vmap(lambda subkey: jax.random.permutation(subkey, TILES))(jax.random.split(keys[8], groups * N_PACK))
    shuffle = shuffle.reshape(groups, N_PACK, TILES).astype(jnp.int32)
    shape_ids = jnp.take_along_axis(shape_ids, shuffle, axis=2)
    return shape_ids.reshape(T_ALL).astype(jnp.int32)


def touch_ends(values, stream_key, smallest, high):
    longest = values.shape.index(max(values.shape))
    spots = []
    for shift in (0, 1):
        where = [jax.random.randint(jax.random.fold_in(stream_key, axis), (), 0, length) for axis, length in enumerate(values.shape)]
        where[longest] = (where[longest] + shift) % values.shape[longest]
        spots.append(tuple(where))
    return values.at[spots[0]].set(smallest).at[spots[1]].set(high)


def steps_of(key, shape, cuts, least, top_value):
    def one(axis_at, blocks):
        heights = jax.random.uniform(jax.random.fold_in(jax.random.fold_in(key, 6), axis_at), (blocks,), jnp.float32, least / len(cuts), top_value / len(cuts))
        return jnp.repeat(jnp.exp(heights), shape[axis_at] // blocks).reshape((-1,) + (1,) * (len(shape) - axis_at - 1))

    factor_of = one(*cuts[0])
    for cut in cuts[1:]:
        factor_of = factor_of * one(*cut)
    return factor_of


def gaussian(key, extent, scale, reach, cuts=(), held_as=jnp.bfloat16):
    entries = jax.random.normal(key, extent, jnp.float32) * scale
    if len(cuts) > 0:
        entries = steps_of(key, extent, cuts, -0.22, 0.18) * entries
    return jnp.clip(entries, min=-reach, max=reach).astype(held_as)


def setup_inputs(seed: int = 0) -> dict:
    seeds = jax.random.split(jax.random.key(seed), 12)
    points = gaussian(seeds[0], (T_ALL * TILE_PTS, CH), 1.0, 6.0, ((0, 1024),))
    neighbours = draw_neighbours(jax.random.fold_in(seeds[11], 71), 0)
    tile_points = draw_tile_points(jax.random.fold_in(seeds[11], 71), 0)
    tile_shape = draw_tile_shape(jax.random.fold_in(seeds[11], 71), 0)
    captions = gaussian(seeds[4], (S_ALL, EMB), 1.0, 6.0, ((0, 1024),))
    positive = touch_ends(jax.random.randint(seeds[5], (S_ALL,), 0, S_DEV * N_BLK), jax.random.fold_in(seeds[5], 1), 0, (S_DEV * N_BLK) - 1).astype(jnp.int32)
    self_weight = gaussian(seeds[6], (CH, CH), CH ** -0.5, 0.375)
    neighbour_weight = gaussian(seeds[7], (CH, CH), CH ** -0.5, 0.375)
    projection = gaussian(seeds[8], (CH, EMB), CH ** -0.5, 0.375)
    logit_scale = jnp.clip(jnp.exp(jax.random.uniform(seeds[9], (1,), jnp.float32, math.log(3.0), math.log(10.0))), 3.0, 10.0)
    logit_bias = jnp.clip(jax.random.uniform(seeds[10], (1,), jnp.float32, -4.0, -1.0), -4.0, -1.0)
    return dict(points=points, neighbours=neighbours, tile_points=tile_points, tile_shape=tile_shape, captions=captions, positive=positive, self_weight=self_weight, neighbour_weight=neighbour_weight, projection=projection, logit_scale=logit_scale, logit_bias=logit_bias)


def encode_block(features, links, counts, self_weight, neighbour_weight):
    positions = jnp.arange(TILE_PTS, dtype=jnp.int32)
    adjacency = lax.optimization_barrier(jnp.sum((links[:, :, :, None] == positions).astype(jnp.float32), axis=1))
    aggregate = (jnp.einsum('mpq,mqc->mpc', adjacency, features.astype(jnp.float32)) / NEIGH).astype(jnp.bfloat16)
    before = jnp.einsum('mpc,cd->mpd', features.astype(jnp.float32), self_weight.astype(jnp.float32))
    before = before + jnp.einsum('mpc,cd->mpd', aggregate.astype(jnp.float32), neighbour_weight.astype(jnp.float32))
    center = before - lax.optimization_barrier(jnp.mean(before, axis=-1, keepdims=True))
    spread = lax.optimization_barrier(jnp.mean(center * center, axis=-1, keepdims=True))
    hidden = features.astype(jnp.float32) + jax.nn.relu(center * lax.rsqrt(spread + 1e-05))
    valid = positions[None, :] < counts[:, None]
    return lax.optimization_barrier(jnp.sum(jnp.where(valid[:, :, None], hidden, 0.0), axis=1))

def grouped(array):
    rest = array.shape[1:]
    shaped = array.reshape((N_DP, N_BLK, N_PACK, S_DEV) + rest)
    moved = jnp.swapaxes(shaped, 1, 2)
    return moved.reshape((N_DP * N_PACK, N_BLK * S_DEV) + rest)

def ungrouped(array):
    rest = array.shape[2:]
    shaped = array.reshape((N_DP, N_PACK, N_BLK, S_DEV) + rest)
    moved = jnp.swapaxes(shaped, 1, 2)
    return moved.reshape((S_ALL,) + rest)

def reference(points, neighbours, tile_points, tile_shape, captions, positive, self_weight, neighbour_weight, projection, logit_scale, logit_bias):
    device_count = N_DP * N_BLK * N_PACK
    features = points.reshape(device_count, TILES, TILE_PTS, CH)
    links = jnp.transpose(neighbours.reshape(NEIGH, device_count, TILES, TILE_PTS), (1, 2, 0, 3))
    counts = tile_points.reshape(device_count, TILES)

    def per_device(items):
        return encode_block(items[0], items[1], items[2], self_weight, neighbour_weight)
    tile_sums = lax.map(per_device, (features, links, counts)).reshape(T_ALL, CH)
    shape_sums = jax.ops.segment_sum(tile_sums, tile_shape, num_segments=S_ALL)
    center = shape_sums - lax.optimization_barrier(jnp.mean(shape_sums, axis=-1, keepdims=True))
    pooled = (center * lax.rsqrt(lax.optimization_barrier(jnp.mean(center * center, axis=-1, keepdims=True)) + 1e-05)).astype(jnp.bfloat16)
    raw_embed = jnp.dot(pooled, projection, preferred_element_type=jnp.float32)
    norms = jnp.sqrt(lax.optimization_barrier(jnp.sum(raw_embed * raw_embed, axis=-1, keepdims=True)) + 1e-06)
    unit_shape = raw_embed / norms
    shape_embed = unit_shape.astype(jnp.bfloat16)
    caption_wide = captions.astype(jnp.float32)
    caption_embed = (caption_wide / jnp.sqrt(lax.optimization_barrier(jnp.sum(caption_wide * caption_wide, axis=-1, keepdims=True)) + 1e-06)).astype(jnp.bfloat16)
    shape_group = grouped(shape_embed).astype(jnp.float32)
    caption_group = grouped(caption_embed).astype(jnp.float32)
    positive_group = grouped(positive)
    scale = logit_scale[0]
    logits = scale * jnp.einsum('gie,gje->gij', shape_group, caption_group) + logit_bias[0]
    columns = jnp.arange(N_BLK * S_DEV, dtype=jnp.int32)
    label = jnp.where(columns[None, None, :] == positive_group[:, :, None], 1.0, -1.0).astype(jnp.float32)
    coef = (-label * jax.nn.sigmoid(-label * logits)).astype(jnp.bfloat16).astype(jnp.float32)
    caption_grad = ungrouped(scale * jnp.einsum('gij,gie->gje', coef, shape_group))
    shape_grad = ungrouped(scale * jnp.einsum('gij,gje->gie', coef, caption_group))
    raw_grad = (shape_grad - unit_shape * lax.optimization_barrier(jnp.sum(unit_shape * shape_grad, axis=-1, keepdims=True))) / norms
    projection_grad = jnp.dot(pooled.astype(jnp.float32).T, raw_grad, precision=lax.Precision.HIGHEST)
    return (caption_grad, projection_grad)
```

```python
import jax
import jax.numpy as jnp
from jax import lax
from jax.experimental import pallas as pl
from jax.experimental.pallas import tpu as pltpu
from jax.sharding import PartitionSpec as P

NEIGH = 27
TILE_PTS = 128
SLOT = 8
STEP_TILES = 3
F32 = jnp.float32
BF16 = jnp.bfloat16
DOT0 = (((0,), (0,)), ((), ()))
DOT1 = (((1,), (1,)), ((), ()))


def encode_kernel(owned, tiles_step, counts, shapes, points, links, self_weight, neighbour_weight, out):
    step = pl.program_id(0)

    @pl.when(step == 0)
    def _():
        out[...] = jnp.zeros_like(out)

    rows = lax.broadcasted_iota(jnp.int32, (TILE_PTS, TILE_PTS), 0)
    valid_rows = lax.broadcasted_iota(jnp.int32, (TILE_PTS, 1), 0)
    for i in range(tiles_step):
        tile = step * tiles_step + i
        span = slice(i * TILE_PTS, (i + 1) * TILE_PTS)
        columns = links[:, span]
        adjacency = jnp.zeros((TILE_PTS, TILE_PTS), F32)
        for k in range(NEIGH):
            adjacency = adjacency + jnp.where(columns[k : k + 1, :] == rows, 1.0, 0.0)
        features = points[span, :]
        aggregate = lax.dot_general(
            adjacency.astype(BF16), features, DOT0, preferred_element_type=F32
        ) * (1.0 / NEIGH)
        before = jnp.dot(features, self_weight[...], preferred_element_type=F32) + jnp.dot(
            aggregate.astype(BF16), neighbour_weight[...], preferred_element_type=F32
        )
        center = before - jnp.mean(before, axis=-1, keepdims=True)
        spread = jnp.mean(center * center, axis=-1, keepdims=True)
        hidden = features.astype(F32) + jnp.maximum(center * lax.rsqrt(spread + 1e-05), 0.0)
        hidden = jnp.where(valid_rows < counts[tile], hidden, 0.0)
        tile_sum = jnp.sum(hidden, axis=0, keepdims=True)
        place = lax.rem(shapes[tile], out.shape[0] // SLOT * owned)
        slot = pl.ds(lax.div(place, owned) * SLOT + lax.rem(place, owned), 1)
        out[slot, :] = out[slot, :] + tile_sum


def encode(points, links, counts, shapes, self_weight, neighbour_weight, packs, owned):
    tiles = counts.shape[0]
    channels = points.shape[1]
    steps = tiles // STEP_TILES
    whole = pl.BlockSpec((channels, channels), lambda i: (0, 0))
    smem = pl.BlockSpec(memory_space=pltpu.SMEM)

    def body(*refs):
        encode_kernel(owned, STEP_TILES, *refs)

    return pl.pallas_call(
        body,
        grid=(steps,),
        out_shape=jax.ShapeDtypeStruct((packs * SLOT, channels), F32),
        in_specs=[
            smem,
            smem,
            pl.BlockSpec((STEP_TILES * TILE_PTS, channels), lambda i: (i, 0)),
            pl.BlockSpec((NEIGH, STEP_TILES * TILE_PTS), lambda i: (0, i)),
            whole,
            whole,
        ],
        out_specs=pl.BlockSpec((packs * SLOT, channels), lambda i: (0, 0)),
        compiler_params=pltpu.CompilerParams(vmem_limit_bytes=24 * 1024 * 1024),
        name="encode",
    )(counts, shapes, points, links, self_weight, neighbour_weight)


def caption_kernel(owned, where, positive, captions, out):
    wide = captions[...].astype(F32)
    unit = wide / jnp.sqrt(jnp.sum(wide * wide, axis=-1, keepdims=True) + 1e-06)
    out[...] = jnp.zeros_like(out)
    out[0:owned, :] = unit
    lanes = lax.broadcasted_iota(jnp.int32, (1, out.shape[1]), 1)
    row = jnp.zeros((1, out.shape[1]), F32)
    for i in range(owned):
        pos = positive[i]
        padded = lax.div(pos, owned) * SLOT + lax.rem(pos, owned)
        row = row + jnp.where(lanes == where[0] * SLOT + i, padded.astype(F32), 0.0)
    out[owned : owned + 1, :] = row


def prepare_captions(captions, positive, blk):
    owned, width = captions.shape
    smem = pl.BlockSpec(memory_space=pltpu.SMEM)

    def body(*refs):
        caption_kernel(owned, *refs)

    return pl.pallas_call(
        body,
        out_shape=jax.ShapeDtypeStruct((SLOT, width), F32),
        in_specs=[smem, smem, pl.BlockSpec(memory_space=pltpu.VMEM)],
        out_specs=pl.BlockSpec(memory_space=pltpu.VMEM),
        name="unit_captions",
    )(blk, positive, captions).astype(BF16)


def loss_kernel(owned, dps, blks, packs, where, scales, sums, captions, projection, caption_grad, rows_grad):
    group = blks * SLOT
    shape_sums = sums[:, 0]
    for p in range(1, packs):
        shape_sums = shape_sums + sums[:, p]
    shape_sums = shape_sums.reshape(group, shape_sums.shape[-1])
    center = shape_sums - jnp.mean(shape_sums, axis=-1, keepdims=True)
    pooled = (center * lax.rsqrt(jnp.mean(center * center, axis=-1, keepdims=True) + 1e-05)).astype(BF16)
    raw_embed = jnp.dot(pooled, projection[...], preferred_element_type=F32)
    norms = jnp.sqrt(jnp.sum(raw_embed * raw_embed, axis=-1, keepdims=True) + 1e-06)
    unit_shape = raw_embed / norms
    shape_embed = unit_shape.astype(BF16)
    given = captions[...].astype(F32)
    slot_rows = lax.rem(lax.broadcasted_iota(jnp.int32, (group, 1), 0), SLOT)
    positive = jnp.sum(jnp.where(slot_rows == owned, given[:, 0:group], 0.0), axis=0, keepdims=True)
    caption_embed = jnp.where(slot_rows < owned, given, 0.0).astype(BF16)
    scale = scales[0]
    logits = scale * lax.dot_general(caption_embed, shape_embed, DOT1, preferred_element_type=F32) + scales[1]
    rows = lax.broadcasted_iota(jnp.int32, (group, group), 0)
    label = jnp.where(rows == positive.astype(jnp.int32), 1.0, -1.0)
    coef = -label * jax.nn.sigmoid(-label * logits)
    mine = lax.broadcasted_iota(jnp.int32, (SLOT, group), 0) + where[0] * SLOT
    pick = jnp.where(mine == lax.broadcasted_iota(jnp.int32, (SLOT, group), 1), 1.0, 0.0).astype(BF16)
    coef = coef.astype(BF16)
    own_coef = jnp.dot(pick, coef, preferred_element_type=F32).astype(BF16)
    own_grad = scale * jnp.dot(own_coef, shape_embed, preferred_element_type=F32)
    caption_grad[...] = own_grad[0:owned, :]
    shape_grad = scale * lax.dot_general(coef, caption_embed, DOT0, preferred_element_type=F32)
    raw_grad = (shape_grad - unit_shape * jnp.sum(unit_shape * shape_grad, axis=-1, keepdims=True)) / norms
    channels = pooled.shape[1]
    each = channels // dps // blks
    kept = lax.broadcasted_iota(jnp.int32, (channels // blks, channels), 0)
    chosen = lax.div(kept, each) * (channels // dps) + lax.rem(kept, each) + where[0] * each
    select = jnp.where(
        chosen == lax.broadcasted_iota(jnp.int32, (channels // blks, channels), 1), 1.0, 0.0
    ).astype(BF16)
    factors = lax.dot_general(select, pooled, DOT1, preferred_element_type=F32).astype(BF16)
    high = raw_grad.astype(BF16)
    low = (raw_grad - high.astype(F32)).astype(BF16)
    rows_grad[...] = jnp.dot(factors, high, preferred_element_type=F32) + jnp.dot(
        factors, low, preferred_element_type=F32
    )


def loss_grads(sums, captions, projection, scales, blk, owned, dps):
    blks, packs = sums.shape[:2]
    channels, width = projection.shape
    smem = pl.BlockSpec(memory_space=pltpu.SMEM)
    vmem = pl.BlockSpec(memory_space=pltpu.VMEM)

    def body(*refs):
        loss_kernel(owned, dps, blks, packs, *refs)

    return pl.pallas_call(
        body,
        out_shape=(
            jax.ShapeDtypeStruct((owned, width), F32),
            jax.ShapeDtypeStruct((channels // blks, width), F32),
        ),
        in_specs=[smem, smem, vmem, vmem, vmem],
        out_specs=(vmem, vmem),
        compiler_params=pltpu.CompilerParams(vmem_limit_bytes=32 * 1024 * 1024),
        name="loss_grads",
    )(blk, scales, sums, captions, projection)


def to_all(array, axes, size):
    copies = jnp.broadcast_to(array[None], (size,) + array.shape)
    return lax.all_to_all(copies, axes, 0, 0, tiled=True)


def shards(
    points,
    neighbours,
    tile_points,
    tile_shape,
    captions,
    positive,
    self_weight,
    neighbour_weight,
    projection,
    logit_scale,
    logit_bias,
):
    owned, width = captions.shape
    channels = points.shape[1]
    packs = lax.axis_size("pack")
    blks = lax.axis_size("blk")
    dps = lax.axis_size("dp")
    blk = lax.axis_index("blk").astype(jnp.int32).reshape(1)
    scales = jnp.concatenate([logit_scale, logit_bias])
    own_captions = prepare_captions(captions, positive, blk)
    all_captions = to_all(own_captions, "blk", blks).reshape(blks * SLOT, width)
    sums = encode(
        points, neighbours, tile_points, tile_shape, self_weight, neighbour_weight, packs, owned
    ).reshape(1, packs, SLOT, channels)
    sums = jnp.broadcast_to(sums, (blks, packs, SLOT, channels))
    sums = lax.all_to_all(
        sums.reshape(blks * packs, SLOT, channels), ("blk", "pack"), 0, 0, tiled=True
    ).reshape(blks, packs, SLOT, channels)
    caption_grad, rows_grad = loss_grads(sums, all_captions, projection, scales, blk, owned, dps)
    rows_grad = lax.all_to_all(rows_grad.reshape(dps, -1, width), "dp", 0, 0, tiled=True)
    row = jnp.sum(rows_grad, axis=0)
    every = to_all(row, ("blk", "pack"), blks * packs)
    projection_grad = jnp.sum(every.reshape(blks, packs, -1, width), axis=1).reshape(-1, width)
    return (caption_grad, projection_grad)


def solution(mesh):
    in_specs = (
        P(("dp", "blk", "pack"), None),
        P(None, ("dp", "blk", "pack")),
        P(("dp", "blk", "pack")),
        P(("dp", "blk", "pack")),
        P(("dp", "blk", "pack"), None),
        P(("dp", "blk", "pack")),
        P(),
        P(),
        P(),
        P(),
        P(),
    )
    out_specs = (P(("dp", "blk", "pack"), None), P("dp", None))
    return jax.shard_map(shards, mesh=mesh, in_specs=in_specs, out_specs=out_specs, check_vma=False)
```

```python
import jax
import jax.numpy as jnp
from jax import lax
from jax.experimental import pallas as pl
from jax.experimental.pallas import tpu as pltpu
from jax.sharding import PartitionSpec as P

NEIGH = 27
TILE_PTS = 128
SLOT = 8
F32 = jnp.float32
BF16 = jnp.bfloat16
DOT0 = (((0,), (0,)), ((), ()))
DOT1 = (((1,), (1,)), ((), ()))


def caption_kernel(owned, blks, where, positive, scale, bias, captions, out, affine):
    affine[0:1, :] = jnp.full((1, affine.shape[1]), scale[0], F32)
    affine[1:2, :] = jnp.full((1, affine.shape[1]), bias[0], F32)
    wide = captions[...].astype(F32)
    unit = wide / jnp.sqrt(jnp.sum(wide * wide, axis=-1, keepdims=True) + 1e-06)
    lanes = lax.broadcasted_iota(jnp.int32, (1, unit.shape[1]), 1)
    row = jnp.zeros((1, unit.shape[1]), F32)
    for i in range(owned):
        place = positive[i]
        padded = lax.div(place, owned) * SLOT + lax.rem(place, owned)
        row = row + jnp.where(lanes == where[0] * SLOT + i, padded.astype(F32), 0.0)
    zeros = jnp.zeros((SLOT - owned - 1, unit.shape[1]), F32)
    block = jnp.concatenate([unit, row, zeros], axis=0)
    pair = jnp.concatenate([block, block], axis=0).astype(BF16)
    for j in range(0, blks * SLOT, 2 * SLOT):
        out[j : j + 2 * SLOT, :] = pair


def unit_captions(blk, positive, scale, bias, captions, blks):
    owned, width = captions.shape
    smem = pl.BlockSpec(memory_space=pltpu.SMEM)
    vmem = pl.BlockSpec(memory_space=pltpu.VMEM)

    def body(*refs):
        caption_kernel(owned, blks, *refs)

    return pl.pallas_call(
        body,
        out_shape=(
            jax.ShapeDtypeStruct((blks * SLOT, width), BF16),
            jax.ShapeDtypeStruct((2, 128), F32),
        ),
        in_specs=[smem, smem, smem, smem, vmem],
        out_specs=(vmem, vmem),
        name="unit_captions",
    )(blk, positive, scale, bias, captions)


def encode_kernel(owned, blks, counts, shapes, points, links, self_weight, neighbour_weight, out, sums):
    tiles = points.shape[0] // TILE_PTS
    rows = lax.broadcasted_iota(jnp.int32, (TILE_PTS, TILE_PTS), 0).astype(F32).astype(BF16)
    ones = jnp.ones((TILE_PTS, TILE_PTS), BF16)
    zeros = jnp.zeros((TILE_PTS, TILE_PTS), BF16)
    aggregates = []
    for tile in range(tiles):
        span = slice(tile * TILE_PTS, (tile + 1) * TILE_PTS)
        columns = links[:, span].astype(F32)
        adjacency = zeros
        for k in range(NEIGH):
            link = jnp.broadcast_to(columns[k : k + 1, :], (16, TILE_PTS)).astype(BF16)
            link = jnp.concatenate([link] * (TILE_PTS // 16), axis=0)
            adjacency = adjacency + jnp.where(link == rows, ones, zeros)
        total = lax.dot_general(adjacency, points[span, :], DOT0, preferred_element_type=F32)
        aggregates.append((total * (1.0 / NEIGH)).astype(BF16))
    features = points[...]
    before = jnp.dot(features, self_weight[...], preferred_element_type=F32) + jnp.dot(
        jnp.concatenate(aggregates, axis=0), neighbour_weight[...], preferred_element_type=F32
    )
    center = before - jnp.mean(before, axis=-1, keepdims=True)
    spread = jnp.mean(center * center, axis=-1, keepdims=True)
    hidden = features.astype(F32) + jnp.maximum(center * lax.rsqrt(spread + 1e-05), 0.0)
    sums[...] = jnp.zeros_like(sums)
    point = lax.broadcasted_iota(jnp.int32, (TILE_PTS, 1), 0)
    for tile in range(tiles):
        span = slice(tile * TILE_PTS, (tile + 1) * TILE_PTS)
        kept = jnp.where(point < counts[tile], hidden[span, :], 0.0)
        place = lax.rem(shapes[tile], sums.shape[0] // SLOT * owned)
        slot = pl.ds(lax.div(place, owned) * SLOT + lax.rem(place, owned), 1)
        sums[slot, :] = sums[slot, :] + jnp.sum(kept, axis=0, keepdims=True)
    total = sums[...]
    for j in range(blks):
        out[j * total.shape[0] : (j + 1) * total.shape[0], :] = total


def encode(counts, shapes, points, links, self_weight, neighbour_weight, blks, packs, owned):
    channels = points.shape[1]
    smem = pl.BlockSpec(memory_space=pltpu.SMEM)
    vmem = pl.BlockSpec(memory_space=pltpu.VMEM)

    def body(*refs):
        encode_kernel(owned, blks, *refs)

    rows = packs * SLOT
    return pl.pallas_call(
        body,
        out_shape=jax.ShapeDtypeStruct((blks * rows, channels), F32),
        in_specs=[smem, smem, vmem, vmem, vmem, vmem],
        out_specs=vmem,
        scratch_shapes=[pltpu.VMEM((rows, channels), F32)],
        compiler_params=pltpu.CompilerParams(vmem_limit_bytes=24 * 1024 * 1024),
        name="encode",
    )(counts, shapes, points, links, self_weight, neighbour_weight)


def loss_kernel(owned, dps, blks, packs, where, affine, sums, captions, projection, caption_grad, rows_grad):
    group = blks * SLOT
    parts = sums[...].reshape(blks, packs, SLOT, sums.shape[-1])
    shape_sums = jnp.sum(parts, axis=1).reshape(group, sums.shape[-1])
    center = shape_sums - jnp.mean(shape_sums, axis=-1, keepdims=True)
    pooled = (center * lax.rsqrt(jnp.mean(center * center, axis=-1, keepdims=True) + 1e-05)).astype(BF16)
    raw_embed = jnp.dot(pooled, projection[...], preferred_element_type=F32)
    norms = jnp.sqrt(jnp.sum(raw_embed * raw_embed, axis=-1, keepdims=True) + 1e-06)
    unit_shape = raw_embed / norms
    shape_embed = unit_shape.astype(BF16)
    given = captions[...].astype(F32)
    slot_rows = lax.rem(lax.broadcasted_iota(jnp.int32, (group, 1), 0), SLOT)
    positive = jnp.sum(jnp.where(slot_rows == owned, given[:, 0:group], 0.0), axis=0, keepdims=True)
    caption_embed = jnp.where(slot_rows < owned, given, 0.0).astype(BF16)
    scale = affine[0:1, 0:1]
    logits = scale * lax.dot_general(caption_embed, shape_embed, DOT1, preferred_element_type=F32) + affine[1:2, 0:1]
    rows = lax.broadcasted_iota(jnp.int32, (group, group), 0)
    label = jnp.where(rows == positive.astype(jnp.int32), 1.0, -1.0)
    coef = -label * jax.nn.sigmoid(-label * logits)
    mine = lax.broadcasted_iota(jnp.int32, (SLOT, group), 0) + where[0] * SLOT
    pick = jnp.where(mine == lax.broadcasted_iota(jnp.int32, (SLOT, group), 1), 1.0, 0.0).astype(BF16)
    coef = coef.astype(BF16)
    own_coef = jnp.dot(pick, coef, preferred_element_type=F32).astype(BF16)
    own_grad = scale * jnp.dot(own_coef, shape_embed, preferred_element_type=F32)
    caption_grad[...] = own_grad[0:owned, :]
    shape_grad = scale * lax.dot_general(coef, caption_embed, DOT0, preferred_element_type=F32)
    raw_grad = (shape_grad - unit_shape * jnp.sum(unit_shape * shape_grad, axis=-1, keepdims=True)) / norms
    channels = pooled.shape[1]
    each = channels // dps // blks
    kept = lax.broadcasted_iota(jnp.int32, (channels // blks, channels), 0)
    chosen = lax.div(kept, each) * (channels // dps) + lax.rem(kept, each) + where[0] * each
    select = jnp.where(
        chosen == lax.broadcasted_iota(jnp.int32, (channels // blks, channels), 1), 1.0, 0.0
    ).astype(BF16)
    factors = lax.dot_general(select, pooled, DOT1, preferred_element_type=F32).astype(BF16)
    high = raw_grad.astype(BF16)
    low = (raw_grad - high.astype(F32)).astype(BF16)
    rows = jnp.dot(factors, high, preferred_element_type=F32) + jnp.dot(
        factors, low, preferred_element_type=F32
    )
    rows_grad[...] = rows.reshape(rows_grad.shape)


def loss_grads(sums, captions, projection, affine, blk, owned, dps, blks, packs):
    channels, width = projection.shape
    smem = pl.BlockSpec(memory_space=pltpu.SMEM)
    vmem = pl.BlockSpec(memory_space=pltpu.VMEM)

    def body(*refs):
        loss_kernel(owned, dps, blks, packs, *refs)

    return pl.pallas_call(
        body,
        out_shape=(
            jax.ShapeDtypeStruct((owned, width), F32),
            jax.ShapeDtypeStruct((dps, channels // dps // blks, width), F32),
        ),
        in_specs=[smem, vmem, vmem, vmem, vmem],
        out_specs=(vmem, vmem),
        compiler_params=pltpu.CompilerParams(vmem_limit_bytes=32 * 1024 * 1024),
        name="loss_grads",
    )(blk, affine, sums, captions, projection)


def sum_packs(every, packs):
    places, each, width = every.shape

    def body(parts, out):
        for b in range(places // packs):
            total = parts[b * packs]
            for p in range(1, packs):
                total = total + parts[b * packs + p]
            out[b * each : (b + 1) * each, :] = total

    vmem = pl.BlockSpec(memory_space=pltpu.VMEM)
    return pl.pallas_call(
        body,
        out_shape=jax.ShapeDtypeStruct((places // packs * each, width), F32),
        in_specs=[vmem],
        out_specs=vmem,
        compiler_params=pltpu.CompilerParams(vmem_limit_bytes=8 * 1024 * 1024),
        name="sum_packs",
    )(every)


def exchange(array, axes, size):
    blocks = array.reshape(size, array.shape[0] // size, array.shape[1])
    return lax.all_to_all(blocks, axes, 0, 0, tiled=True).reshape(array.shape)


def to_all(array, axes, size):
    copies = jnp.broadcast_to(array[None], (size,) + array.shape)
    return lax.all_to_all(copies, axes, 0, 0, tiled=True)


def shards(
    points,
    neighbours,
    tile_points,
    tile_shape,
    captions,
    positive,
    self_weight,
    neighbour_weight,
    projection,
    logit_scale,
    logit_bias,
):
    owned, width = captions.shape
    channels = points.shape[1]
    packs = lax.axis_size("pack")
    blks = lax.axis_size("blk")
    dps = lax.axis_size("dp")
    blk = lax.axis_index("blk").astype(jnp.int32).reshape(1)
    units, affine = unit_captions(blk, positive, logit_scale, logit_bias, captions, blks)
    units = exchange(units, "blk", blks)
    sums = encode(
        tile_points, tile_shape, points, neighbours, self_weight, neighbour_weight, blks, packs, owned
    )
    sums = exchange(sums, ("blk", "pack"), blks * packs)
    caption_grad, rows_grad = loss_grads(
        sums, units, projection, affine, blk, owned, dps, blks, packs
    )
    rows_grad = lax.all_to_all(rows_grad, "dp", 0, 0, tiled=True)
    every = to_all(jnp.sum(rows_grad, axis=0), ("blk", "pack"), blks * packs)
    projection_grad = sum_packs(every, packs)
    return (caption_grad, projection_grad)


def solution(mesh):
    in_specs = (
        P(("dp", "blk", "pack"), None),
        P(None, ("dp", "blk", "pack")),
        P(("dp", "blk", "pack")),
        P(("dp", "blk", "pack")),
        P(("dp", "blk", "pack"), None),
        P(("dp", "blk", "pack")),
        P(),
        P(),
        P(),
        P(),
        P(),
    )
    out_specs = (P(("dp", "blk", "pack"), None), P("dp", None))
    return jax.shard_map(shards, mesh=mesh, in_specs=in_specs, out_specs=out_specs, check_vma=False)
```

```python
import jax
import jax.numpy as jnp
from jax import lax
from jax.experimental import pallas as pl
from jax.experimental.pallas import tpu as pltpu
from jax.sharding import PartitionSpec as P

NEIGH = 27
TILE_PTS = 128
SLOT = 8
ENCODE_VMEM = 60 * 1024 * 1024
F32 = jnp.float32
BF16 = jnp.bfloat16
DOT0 = (((0,), (0,)), ((), ()))
DOT1 = (((1,), (1,)), ((), ()))


def encode_kernel(
    owned,
    counts,
    shapes,
    where,
    scale,
    bias,
    points_far,
    links_far,
    self_far,
    neighbour_far,
    sums,
    points,
    links,
    self_weight,
    neighbour_weight,
    arrived,
):
    copies = [
        pltpu.make_async_copy(far, near, arrived.at[i])
        for i, (far, near) in enumerate(
            (
                (links_far, links),
                (points_far, points),
                (self_far, self_weight),
                (neighbour_far, neighbour_weight),
            )
        )
    ]
    for copy in copies:
        copy.start()
    sums[...] = jnp.zeros_like(sums)
    tiles = points.shape[0] // TILE_PTS
    rows = lax.broadcasted_iota(jnp.int32, (TILE_PTS, TILE_PTS), 0).astype(F32).astype(BF16)
    ones = jnp.ones((TILE_PTS, TILE_PTS), BF16)
    zeros = jnp.zeros((TILE_PTS, TILE_PTS), BF16)
    copies[0].wait()
    adjacencies = []
    for tile in range(tiles):
        columns = links[:, tile * TILE_PTS : (tile + 1) * TILE_PTS].astype(F32)
        adjacency = zeros
        for k in range(NEIGH):
            link = jnp.broadcast_to(columns[k : k + 1, :], (16, TILE_PTS)).astype(BF16)
            link = jnp.concatenate([link] * (TILE_PTS // 16), axis=0)
            adjacency = adjacency + jnp.where(link == rows, ones, zeros)
        adjacencies.append(adjacency)
    for copy in copies[1:]:
        copy.wait()
    aggregates = []
    for tile in range(tiles):
        span = slice(tile * TILE_PTS, (tile + 1) * TILE_PTS)
        total = lax.dot_general(adjacencies[tile], points[span, :], DOT0, preferred_element_type=F32)
        aggregates.append((total * (1.0 / NEIGH)).astype(BF16))
    features = points[...]
    before = jnp.dot(features, self_weight[...], preferred_element_type=F32) + jnp.dot(
        jnp.concatenate(aggregates, axis=0), neighbour_weight[...], preferred_element_type=F32
    )
    center = before - jnp.mean(before, axis=-1, keepdims=True)
    spread = jnp.mean(center * center, axis=-1, keepdims=True)
    hidden = features.astype(F32) + jnp.maximum(center * lax.rsqrt(spread + 1e-05), 0.0)
    point = lax.broadcasted_iota(jnp.int32, (TILE_PTS, 1), 0)
    for tile in range(tiles):
        span = slice(tile * TILE_PTS, (tile + 1) * TILE_PTS)
        kept = jnp.where(point < counts[tile], hidden[span, :], 0.0)
        place = lax.rem(shapes[tile], sums.shape[0] // SLOT * owned)
        slot = pl.ds(lax.div(place, owned) * SLOT + lax.rem(place, owned), 1)
        sums[slot, :] = sums[slot, :] + jnp.sum(kept, axis=0, keepdims=True)


def encode(counts, shapes, blk, scale, bias, points, links, self_weight, neighbour_weight, packs, owned):
    channels = points.shape[1]
    smem = pl.BlockSpec(memory_space=pltpu.SMEM)
    vmem = pl.BlockSpec(memory_space=pltpu.VMEM)
    far = pl.BlockSpec(memory_space=pl.ANY)

    def body(*refs):
        encode_kernel(owned, *refs)

    return pl.pallas_call(
        body,
        out_shape=jax.ShapeDtypeStruct((packs * SLOT, channels), F32),
        in_specs=[smem, smem, smem, smem, smem, far, far, far, far],
        out_specs=vmem,
        scratch_shapes=[
            pltpu.VMEM(points.shape, points.dtype),
            pltpu.VMEM(links.shape, links.dtype),
            pltpu.VMEM(self_weight.shape, self_weight.dtype),
            pltpu.VMEM(neighbour_weight.shape, neighbour_weight.dtype),
            pltpu.SemaphoreType.DMA((4,)),
        ],
        compiler_params=pltpu.CompilerParams(vmem_limit_bytes=ENCODE_VMEM),
        name="encode",
    )(counts, shapes, blk, scale, bias, points, links, self_weight, neighbour_weight)


def pool_kernel(owned, blks, packs, where, positive, sums, captions, out):
    channels = sums.shape[1]
    wide = captions[...].astype(F32)
    unit = wide / jnp.sqrt(jnp.sum(wide * wide, axis=-1, keepdims=True) + 1e-06)
    shape_sums = sums[0:SLOT, :]
    for p in range(1, packs):
        shape_sums = shape_sums + sums[p * SLOT : (p + 1) * SLOT, :]
    center = shape_sums - jnp.mean(shape_sums, axis=-1, keepdims=True)
    pooled = center * lax.rsqrt(jnp.mean(center * center, axis=-1, keepdims=True) + 1e-05)
    across = unit.shape[1] // channels
    lanes = lax.broadcasted_iota(jnp.int32, (1, unit.shape[1] - channels), 1)
    places = jnp.zeros(lanes.shape, F32)
    for i in range(owned):
        place = positive[i]
        padded = lax.div(place, owned) * SLOT + lax.rem(place, owned)
        places = places + jnp.where(lanes == i * blks + where[0], padded.astype(F32), 0.0)
    first = jnp.concatenate([pooled[i : i + 1, :] for i in range(across)], axis=1)
    second = jnp.concatenate([pooled[across : across + 1, :], places], axis=1)
    block = jnp.concatenate([unit, first, second], axis=0)
    pair = jnp.concatenate([block, block], axis=0).astype(BF16)
    for j in range(0, blks * SLOT, 2 * SLOT):
        out[j : j + 2 * SLOT, :] = pair


def pool(blk, positive, sums, captions, blks, packs):
    owned, width = captions.shape
    smem = pl.BlockSpec(memory_space=pltpu.SMEM)
    vmem = pl.BlockSpec(memory_space=pltpu.VMEM)

    def body(*refs):
        pool_kernel(owned, blks, packs, *refs)

    return pl.pallas_call(
        body,
        out_shape=jax.ShapeDtypeStruct((blks * SLOT, width), BF16),
        in_specs=[smem, smem, vmem, vmem],
        out_specs=vmem,
        compiler_params=pltpu.CompilerParams(vmem_limit_bytes=8 * 1024 * 1024),
        name="pool",
    )(blk, positive, sums, captions)


def loss_kernel(owned, dps, blks, where, scale, bias, group_rows, projection, caption_grad, rows_grad):
    group = blks * SLOT
    channels, width = projection.shape
    given = group_rows[...]
    wanted = lax.broadcasted_iota(jnp.int32, (2 * blks, group), 0)
    wanted = lax.rem(wanted, blks) * SLOT + owned + lax.div(wanted, blks)
    lanes = lax.broadcasted_iota(jnp.int32, (2 * blks, group), 1)
    picked = jnp.dot(
        jnp.where(wanted == lanes, 1.0, 0.0).astype(BF16), given, preferred_element_type=F32
    )
    across = width // channels
    pooled = jnp.concatenate(
        [picked[0:blks, i * channels : (i + 1) * channels] for i in range(across)]
        + [picked[blks : 2 * blks, 0:channels]],
        axis=0,
    ).astype(BF16)
    positive = jnp.sum(
        picked[blks : 2 * blks, channels : channels + owned * blks], axis=0, keepdims=True
    ).astype(jnp.int32)
    raw_embed = jnp.dot(pooled, projection[...], preferred_element_type=F32)
    norms = jnp.sqrt(jnp.sum(raw_embed * raw_embed, axis=-1, keepdims=True) + 1e-06)
    unit_shape = raw_embed / norms
    shape_embed = unit_shape.astype(BF16)
    slot_rows = lax.rem(lax.broadcasted_iota(jnp.int32, (group, 1), 0), SLOT)
    caption_embed = jnp.where(slot_rows < owned, given.astype(F32), 0.0).astype(BF16)
    logits = (
        scale[0] * lax.dot_general(caption_embed, shape_embed, DOT1, preferred_element_type=F32)
        + bias[0]
    )
    rows = lax.broadcasted_iota(jnp.int32, logits.shape, 0)
    label = jnp.where(rows == positive, 1.0, -1.0)
    coef = (-label * jax.nn.sigmoid(-label * logits)).astype(BF16)
    mine = lax.broadcasted_iota(jnp.int32, (SLOT, group), 0) + where[0] * SLOT
    pick = jnp.where(mine == lax.broadcasted_iota(jnp.int32, (SLOT, group), 1), 1.0, 0.0).astype(BF16)
    own_coef = jnp.dot(pick, coef, preferred_element_type=F32).astype(BF16)
    own_grad = scale[0] * jnp.dot(own_coef, shape_embed, preferred_element_type=F32)
    caption_grad[...] = own_grad[0:owned, :]
    shape_grad = scale[0] * lax.dot_general(coef, caption_embed, DOT0, preferred_element_type=F32)
    raw_grad = (shape_grad - unit_shape * jnp.sum(unit_shape * shape_grad, axis=-1, keepdims=True)) / norms
    each = channels // dps // blks
    kept = lax.broadcasted_iota(jnp.int32, (channels // blks, channels), 0)
    chosen = lax.div(kept, each) * (channels // dps) + lax.rem(kept, each) + where[0] * each
    select = jnp.where(
        chosen == lax.broadcasted_iota(jnp.int32, (channels // blks, channels), 1), 1.0, 0.0
    ).astype(BF16)
    factors = lax.dot_general(select, pooled, DOT1, preferred_element_type=F32).astype(BF16)
    high = raw_grad.astype(BF16)
    low = (raw_grad - high.astype(F32)).astype(BF16)
    rows = jnp.dot(factors, high, preferred_element_type=F32) + jnp.dot(
        factors, low, preferred_element_type=F32
    )
    rows_grad[...] = rows.reshape(rows_grad.shape)


def loss_grads(blk, scale, bias, group_rows, projection, owned, dps, blks):
    channels, width = projection.shape
    smem = pl.BlockSpec(memory_space=pltpu.SMEM)
    vmem = pl.BlockSpec(memory_space=pltpu.VMEM)

    def body(*refs):
        loss_kernel(owned, dps, blks, *refs)

    return pl.pallas_call(
        body,
        out_shape=(
            jax.ShapeDtypeStruct((owned, width), F32),
            jax.ShapeDtypeStruct((dps, channels // dps // blks, width), F32),
        ),
        in_specs=[smem, smem, smem, vmem, vmem],
        out_specs=(vmem, vmem),
        compiler_params=pltpu.CompilerParams(vmem_limit_bytes=32 * 1024 * 1024),
        name="loss_grads",
    )(blk, scale, bias, group_rows, projection)


def sum_packs(every, packs):
    places, each, width = every.shape

    def body(parts, out):
        for b in range(places // packs):
            total = parts[b * packs]
            for p in range(1, packs):
                total = total + parts[b * packs + p]
            out[b * each : (b + 1) * each, :] = total

    vmem = pl.BlockSpec(memory_space=pltpu.VMEM)
    return pl.pallas_call(
        body,
        out_shape=jax.ShapeDtypeStruct((places // packs * each, width), F32),
        in_specs=[vmem],
        out_specs=vmem,
        compiler_params=pltpu.CompilerParams(vmem_limit_bytes=8 * 1024 * 1024),
        name="sum_packs",
    )(every)


def exchange(array, axes, size):
    blocks = array.reshape(size, array.shape[0] // size, array.shape[1])
    return lax.all_to_all(blocks, axes, 0, 0, tiled=True).reshape(array.shape)


def to_all(array, axes, size):
    copies = jnp.broadcast_to(array[None], (size,) + array.shape)
    return lax.all_to_all(copies, axes, 0, 0, tiled=True)


def shards(
    points,
    neighbours,
    tile_points,
    tile_shape,
    captions,
    positive,
    self_weight,
    neighbour_weight,
    projection,
    logit_scale,
    logit_bias,
):
    owned = captions.shape[0]
    packs = lax.axis_size("pack")
    blks = lax.axis_size("blk")
    dps = lax.axis_size("dp")
    blk = lax.axis_index("blk").astype(jnp.int32).reshape(1)
    sums = encode(
        tile_points,
        tile_shape,
        blk,
        logit_scale,
        logit_bias,
        points,
        neighbours,
        self_weight,
        neighbour_weight,
        packs,
        owned,
    )
    sums = exchange(sums, "pack", packs)
    group_rows = exchange(pool(blk, positive, sums, captions, blks, packs), "blk", blks)
    caption_grad, rows_grad = loss_grads(
        blk,
        logit_scale,
        logit_bias,
        group_rows,
        projection,
        owned,
        dps,
        blks,
    )
    rows_grad = lax.all_to_all(rows_grad, "dp", 0, 0, tiled=True)
    every = to_all(jnp.sum(rows_grad, axis=0), ("blk", "pack"), blks * packs)
    projection_grad = sum_packs(every, packs)
    return (caption_grad, projection_grad)


def solution(mesh):
    in_specs = (
        P(("dp", "blk", "pack"), None),
        P(None, ("dp", "blk", "pack")),
        P(("dp", "blk", "pack")),
        P(("dp", "blk", "pack")),
        P(("dp", "blk", "pack"), None),
        P(("dp", "blk", "pack")),
        P(),
        P(),
        P(),
        P(),
        P(),
    )
    out_specs = (P(("dp", "blk", "pack"), None), P("dp", None))
    return jax.shard_map(shards, mesh=mesh, in_specs=in_specs, out_specs=out_specs, check_vma=False)
```

```python
import jax
import jax.numpy as jnp
from jax import lax
from jax.experimental import pallas as pl
from jax.experimental.pallas import tpu as pltpu
from jax.sharding import PartitionSpec as P

NEIGH = 27
TILE_PTS = 128
SLOT = 8
ENCODE_VMEM = 60 * 1024 * 1024
F32 = jnp.float32
BF16 = jnp.bfloat16
DOT0 = (((0,), (0,)), ((), ()))
DOT1 = (((1,), (1,)), ((), ()))


def encode_kernel(
    owned,
    scale,
    bias,
    counts_far,
    shapes_far,
    points_far,
    links_far,
    self_far,
    neighbour_far,
    sums,
    counts,
    shapes,
    points,
    links,
    self_weight,
    neighbour_weight,
    arrived,
):
    copies = [
        pltpu.make_async_copy(far, near, arrived.at[i])
        for i, (far, near) in enumerate(
            (
                (links_far, links),
                (points_far, points),
                (self_far, self_weight),
                (neighbour_far, neighbour_weight),
                (counts_far, counts),
                (shapes_far, shapes),
            )
        )
    ]
    for copy in copies:
        copy.start()
    sums[...] = jnp.zeros_like(sums)
    tiles = points.shape[0] // TILE_PTS
    rows = lax.broadcasted_iota(jnp.int32, (TILE_PTS, TILE_PTS), 0).astype(F32).astype(BF16)
    ones = jnp.ones((TILE_PTS, TILE_PTS), BF16)
    zeros = jnp.zeros((TILE_PTS, TILE_PTS), BF16)
    copies[0].wait()
    adjacencies = []
    for tile in range(tiles):
        columns = links[:, tile * TILE_PTS : (tile + 1) * TILE_PTS].astype(F32)
        adjacency = zeros
        for k in range(NEIGH):
            link = jnp.broadcast_to(columns[k : k + 1, :], (16, TILE_PTS)).astype(BF16)
            link = jnp.concatenate([link] * (TILE_PTS // 16), axis=0)
            adjacency = adjacency + jnp.where(link == rows, ones, zeros)
        adjacencies.append(adjacency)
    for copy in copies[1:]:
        copy.wait()
    aggregates = []
    for tile in range(tiles):
        span = slice(tile * TILE_PTS, (tile + 1) * TILE_PTS)
        total = lax.dot_general(adjacencies[tile], points[span, :], DOT0, preferred_element_type=F32)
        aggregates.append((total * (1.0 / NEIGH)).astype(BF16))
    features = points[...]
    before = jnp.dot(features, self_weight[...], preferred_element_type=F32) + jnp.dot(
        jnp.concatenate(aggregates, axis=0), neighbour_weight[...], preferred_element_type=F32
    )
    center = before - jnp.mean(before, axis=-1, keepdims=True)
    spread = jnp.mean(center * center, axis=-1, keepdims=True)
    hidden = features.astype(F32) + jnp.maximum(center * lax.rsqrt(spread + 1e-05), 0.0)
    point = lax.broadcasted_iota(jnp.int32, (TILE_PTS, 1), 0)
    for tile in range(tiles):
        span = slice(tile * TILE_PTS, (tile + 1) * TILE_PTS)
        kept = jnp.where(point < counts[tile], hidden[span, :], 0.0)
        place = lax.rem(shapes[tile], sums.shape[0] // SLOT * owned)
        slot = pl.ds(lax.div(place, owned) * SLOT + lax.rem(place, owned), 1)
        sums[slot, :] = sums[slot, :] + jnp.sum(kept, axis=0, keepdims=True)


def encode(scale, bias, counts, shapes, points, links, self_weight, neighbour_weight, packs, owned):
    channels = points.shape[1]
    smem = pl.BlockSpec(memory_space=pltpu.SMEM)
    vmem = pl.BlockSpec(memory_space=pltpu.VMEM)
    far = pl.BlockSpec(memory_space=pl.ANY)

    def body(*refs):
        encode_kernel(owned, *refs)

    return pl.pallas_call(
        body,
        out_shape=jax.ShapeDtypeStruct((packs * SLOT, channels), F32),
        in_specs=[smem] * 2 + [far] * 6,
        out_specs=vmem,
        scratch_shapes=[
            pltpu.SMEM(counts.shape, counts.dtype),
            pltpu.SMEM(shapes.shape, shapes.dtype),
            pltpu.VMEM(points.shape, points.dtype),
            pltpu.VMEM(links.shape, links.dtype),
            pltpu.VMEM(self_weight.shape, self_weight.dtype),
            pltpu.VMEM(neighbour_weight.shape, neighbour_weight.dtype),
            pltpu.SemaphoreType.DMA((6,)),
        ],
        compiler_params=pltpu.CompilerParams(vmem_limit_bytes=ENCODE_VMEM),
        name="encode",
    )(scale, bias, counts, shapes, points, links, self_weight, neighbour_weight)


def pool_kernel(owned, blks, packs, positive, sums, captions, out):
    where = lax.axis_index("blk")
    channels = sums.shape[1]
    wide = captions[...].astype(F32)
    unit = wide / jnp.sqrt(jnp.sum(wide * wide, axis=-1, keepdims=True) + 1e-06)
    shape_sums = sums[0:SLOT, :]
    for p in range(1, packs):
        shape_sums = shape_sums + sums[p * SLOT : (p + 1) * SLOT, :]
    center = shape_sums - jnp.mean(shape_sums, axis=-1, keepdims=True)
    pooled = center * lax.rsqrt(jnp.mean(center * center, axis=-1, keepdims=True) + 1e-05)
    across = unit.shape[1] // channels
    lanes = lax.broadcasted_iota(jnp.int32, (1, unit.shape[1] - channels), 1)
    places = jnp.zeros(lanes.shape, F32)
    for i in range(owned):
        place = positive[i]
        padded = lax.div(place, owned) * SLOT + lax.rem(place, owned)
        places = places + jnp.where(lanes == i * blks + where, padded.astype(F32), 0.0)
    first = jnp.concatenate([pooled[i : i + 1, :] for i in range(across)], axis=1)
    second = jnp.concatenate([pooled[across : across + 1, :], places], axis=1)
    block = jnp.concatenate([unit, first, second], axis=0)
    pair = jnp.concatenate([block, block], axis=0).astype(BF16)
    for j in range(0, blks * SLOT, 2 * SLOT):
        out[j : j + 2 * SLOT, :] = pair


def pool(positive, sums, captions, blks, packs):
    owned, width = captions.shape
    smem = pl.BlockSpec(memory_space=pltpu.SMEM)
    vmem = pl.BlockSpec(memory_space=pltpu.VMEM)

    def body(*refs):
        pool_kernel(owned, blks, packs, *refs)

    return pl.pallas_call(
        body,
        out_shape=jax.ShapeDtypeStruct((blks * SLOT, width), BF16),
        in_specs=[smem, vmem, vmem],
        out_specs=vmem,
        compiler_params=pltpu.CompilerParams(vmem_limit_bytes=8 * 1024 * 1024),
        name="pool",
    )(positive, sums, captions)


def loss_kernel(owned, dps, blks, scale, bias, group_rows, projection, caption_grad, rows_grad):
    where = lax.axis_index("blk")
    group = blks * SLOT
    channels, width = projection.shape
    given = group_rows[...]
    wanted = lax.broadcasted_iota(jnp.int32, (2 * blks, group), 0)
    wanted = lax.rem(wanted, blks) * SLOT + owned + lax.div(wanted, blks)
    lanes = lax.broadcasted_iota(jnp.int32, (2 * blks, group), 1)
    picked = jnp.dot(
        jnp.where(wanted == lanes, 1.0, 0.0).astype(BF16), given, preferred_element_type=F32
    )
    across = width // channels
    pooled = jnp.concatenate(
        [picked[0:blks, i * channels : (i + 1) * channels] for i in range(across)]
        + [picked[blks : 2 * blks, 0:channels]],
        axis=0,
    ).astype(BF16)
    positive = jnp.sum(
        picked[blks : 2 * blks, channels : channels + owned * blks], axis=0, keepdims=True
    ).astype(jnp.int32)
    raw_embed = jnp.dot(pooled, projection[...], preferred_element_type=F32)
    norms = jnp.sqrt(jnp.sum(raw_embed * raw_embed, axis=-1, keepdims=True) + 1e-06)
    unit_shape = raw_embed / norms
    shape_embed = unit_shape.astype(BF16)
    logits = (
        scale[0] * lax.dot_general(given, shape_embed, DOT1, preferred_element_type=F32)
        + bias[0]
    )
    rows = lax.broadcasted_iota(jnp.int32, logits.shape, 0)
    label = jnp.where(rows == positive, 1.0, -1.0)
    coef = -label * jax.nn.sigmoid(-label * logits)
    coef = jnp.where(lax.rem(rows, SLOT) < owned, coef, 0.0).astype(BF16)
    mine = lax.broadcasted_iota(jnp.int32, (SLOT, group), 0) + where * SLOT
    pick = jnp.where(mine == lax.broadcasted_iota(jnp.int32, (SLOT, group), 1), 1.0, 0.0).astype(BF16)
    own_coef = jnp.dot(pick, coef, preferred_element_type=F32).astype(BF16)
    own_grad = scale[0] * jnp.dot(own_coef, shape_embed, preferred_element_type=F32)
    caption_grad[...] = own_grad[0:owned, :]
    shape_grad = scale[0] * lax.dot_general(coef, given, DOT0, preferred_element_type=F32)
    raw_grad = (shape_grad - unit_shape * jnp.sum(unit_shape * shape_grad, axis=-1, keepdims=True)) / norms
    each = channels // dps // blks
    kept = lax.broadcasted_iota(jnp.int32, (channels // blks, channels), 0)
    chosen = lax.div(kept, each) * (channels // dps) + lax.rem(kept, each) + where * each
    select = jnp.where(
        chosen == lax.broadcasted_iota(jnp.int32, (channels // blks, channels), 1), 1.0, 0.0
    ).astype(BF16)
    factors = lax.dot_general(select, pooled, DOT1, preferred_element_type=F32).astype(BF16)
    high = raw_grad.astype(BF16)
    low = (raw_grad - high.astype(F32)).astype(BF16)
    rows = jnp.dot(factors, high, preferred_element_type=F32) + jnp.dot(
        factors, low, preferred_element_type=F32
    )
    rows_grad[...] = rows.reshape(rows_grad.shape)


def loss_grads(scale, bias, group_rows, projection, owned, dps, blks):
    channels, width = projection.shape
    vmem = pl.BlockSpec(memory_space=pltpu.VMEM)
    smem = pl.BlockSpec(memory_space=pltpu.SMEM)

    def body(*refs):
        loss_kernel(owned, dps, blks, *refs)

    return pl.pallas_call(
        body,
        out_shape=(
            jax.ShapeDtypeStruct((owned, width), F32),
            jax.ShapeDtypeStruct((dps, channels // dps // blks, width), F32),
        ),
        in_specs=[smem, smem, vmem, vmem],
        out_specs=(vmem, vmem),
        compiler_params=pltpu.CompilerParams(vmem_limit_bytes=32 * 1024 * 1024),
        name="loss_grads",
    )(scale, bias, group_rows, projection)


def sum_packs(every, packs):
    places, each, width = every.shape

    def body(parts, out):
        for b in range(places // packs):
            total = parts[b * packs]
            for p in range(1, packs):
                total = total + parts[b * packs + p]
            out[b * each : (b + 1) * each, :] = total

    vmem = pl.BlockSpec(memory_space=pltpu.VMEM)
    return pl.pallas_call(
        body,
        out_shape=jax.ShapeDtypeStruct((places // packs * each, width), F32),
        in_specs=[vmem],
        out_specs=vmem,
        compiler_params=pltpu.CompilerParams(vmem_limit_bytes=8 * 1024 * 1024),
        name="sum_packs",
    )(every)


def exchange(array, axes, size):
    blocks = array.reshape(size, array.shape[0] // size, array.shape[1])
    return lax.all_to_all(blocks, axes, 0, 0, tiled=True).reshape(array.shape)


def to_all(array, axes, size):
    copies = jnp.broadcast_to(array[None], (size,) + array.shape)
    return lax.all_to_all(copies, axes, 0, 0, tiled=True)


def shards(
    points,
    neighbours,
    tile_points,
    tile_shape,
    captions,
    positive,
    self_weight,
    neighbour_weight,
    projection,
    logit_scale,
    logit_bias,
):
    owned = captions.shape[0]
    packs = lax.axis_size("pack")
    blks = lax.axis_size("blk")
    dps = lax.axis_size("dp")
    sums = encode(
        logit_scale,
        logit_bias,
        tile_points,
        tile_shape,
        points,
        neighbours,
        self_weight,
        neighbour_weight,
        packs,
        owned,
    )
    sums = exchange(sums, "pack", packs)
    group_rows = exchange(pool(positive, sums, captions, blks, packs), "blk", blks)
    caption_grad, rows_grad = loss_grads(
        logit_scale,
        logit_bias,
        group_rows,
        projection,
        owned,
        dps,
        blks,
    )
    rows_grad = lax.all_to_all(rows_grad, "dp", 0, 0, tiled=True)
    every = to_all(jnp.sum(rows_grad, axis=0), ("blk", "pack"), blks * packs)
    projection_grad = sum_packs(every, packs)
    return (caption_grad, projection_grad)


def solution(mesh):
    in_specs = (
        P(("dp", "blk", "pack"), None),
        P(None, ("dp", "blk", "pack")),
        P(("dp", "blk", "pack")),
        P(("dp", "blk", "pack")),
        P(("dp", "blk", "pack"), None),
        P(("dp", "blk", "pack")),
        P(),
        P(),
        P(),
        P(),
        P(),
    )
    out_specs = (P(("dp", "blk", "pack"), None), P("dp", None))
    return jax.shard_map(shards, mesh=mesh, in_specs=in_specs, out_specs=out_specs, check_vma=False)
```

```python
import jax
import jax.numpy as jnp
from jax import lax
from jax.experimental import pallas as pl
from jax.experimental.pallas import tpu as pltpu
from jax.sharding import PartitionSpec as P

NEIGH = 27
TILE_PTS = 128
SLOT = 8
ENCODE_VMEM = 60 * 1024 * 1024
F32 = jnp.float32
BF16 = jnp.bfloat16
DOT0 = (((0,), (0,)), ((), ()))
DOT1 = (((1,), (1,)), ((), ()))


def encode_kernel(
    owned,
    scale,
    bias,
    counts_far,
    shapes_far,
    points_far,
    links_far,
    self_far,
    neighbour_far,
    sums,
    counts,
    shapes,
    points,
    links,
    self_weight,
    neighbour_weight,
    arrived,
):
    copies = [
        pltpu.make_async_copy(far, near, arrived.at[i])
        for i, (far, near) in enumerate(
            (
                (links_far, links),
                (points_far, points),
                (self_far, self_weight),
                (neighbour_far, neighbour_weight),
                (counts_far, counts),
                (shapes_far, shapes),
            )
        )
    ]
    for copy in copies:
        copy.start()
    sums[...] = jnp.zeros_like(sums)
    tiles = points.shape[0] // TILE_PTS
    rows = lax.broadcasted_iota(jnp.int32, (TILE_PTS, TILE_PTS), 0).astype(F32).astype(BF16)
    ones = jnp.ones((TILE_PTS, TILE_PTS), BF16)
    zeros = jnp.zeros((TILE_PTS, TILE_PTS), BF16)
    copies[0].wait()
    adjacencies = []
    for tile in range(tiles):
        columns = links[:, tile * TILE_PTS : (tile + 1) * TILE_PTS].astype(F32)
        adjacency = zeros
        for k in range(NEIGH):
            link = jnp.broadcast_to(columns[k : k + 1, :], (16, TILE_PTS)).astype(BF16)
            link = jnp.concatenate([link] * (TILE_PTS // 16), axis=0)
            adjacency = adjacency + jnp.where(link == rows, ones, zeros)
        adjacencies.append(adjacency)
    for copy in copies[1:]:
        copy.wait()
    aggregates = []
    for tile in range(tiles):
        span = slice(tile * TILE_PTS, (tile + 1) * TILE_PTS)
        total = lax.dot_general(adjacencies[tile], points[span, :], DOT0, preferred_element_type=F32)
        aggregates.append((total * (1.0 / NEIGH)).astype(BF16))
    features = points[...]
    before = jnp.dot(features, self_weight[...], preferred_element_type=F32) + jnp.dot(
        jnp.concatenate(aggregates, axis=0), neighbour_weight[...], preferred_element_type=F32
    )
    center = before - jnp.mean(before, axis=-1, keepdims=True)
    spread = jnp.mean(center * center, axis=-1, keepdims=True)
    hidden = features.astype(F32) + jnp.maximum(center * lax.rsqrt(spread + 1e-05), 0.0)
    point = lax.broadcasted_iota(jnp.int32, (TILE_PTS, 1), 0)
    for tile in range(tiles):
        span = slice(tile * TILE_PTS, (tile + 1) * TILE_PTS)
        kept = jnp.where(point < counts[tile], hidden[span, :], 0.0)
        place = lax.rem(shapes[tile], sums.shape[0] // SLOT * owned)
        slot = pl.ds(lax.div(place, owned) * SLOT + lax.rem(place, owned), 1)
        sums[slot, :] = sums[slot, :] + jnp.sum(kept, axis=0, keepdims=True)


def encode(scale, bias, counts, shapes, points, links, self_weight, neighbour_weight, packs, owned):
    channels = points.shape[1]
    smem = pl.BlockSpec(memory_space=pltpu.SMEM)
    vmem = pl.BlockSpec(memory_space=pltpu.VMEM)
    far = pl.BlockSpec(memory_space=pl.ANY)

    def body(*refs):
        encode_kernel(owned, *refs)

    return pl.pallas_call(
        body,
        out_shape=jax.ShapeDtypeStruct((packs * SLOT, channels), F32),
        in_specs=[smem] * 2 + [far] * 6,
        out_specs=vmem,
        scratch_shapes=[
            pltpu.SMEM(counts.shape, counts.dtype),
            pltpu.SMEM(shapes.shape, shapes.dtype),
            pltpu.VMEM(points.shape, points.dtype),
            pltpu.VMEM(links.shape, links.dtype),
            pltpu.VMEM(self_weight.shape, self_weight.dtype),
            pltpu.VMEM(neighbour_weight.shape, neighbour_weight.dtype),
            pltpu.SemaphoreType.DMA((6,)),
        ],
        compiler_params=pltpu.CompilerParams(vmem_limit_bytes=ENCODE_VMEM),
        name="encode",
    )(scale, bias, counts, shapes, points, links, self_weight, neighbour_weight)


def pool_kernel(owned, blks, packs, positive, sums, captions, out):
    where = lax.axis_index("blk")
    channels = sums.shape[1]
    wide = captions[...].astype(F32)
    unit = wide / jnp.sqrt(jnp.sum(wide * wide, axis=-1, keepdims=True) + 1e-06)
    shape_sums = sums[0:SLOT, :]
    for p in range(1, packs):
        shape_sums = shape_sums + sums[p * SLOT : (p + 1) * SLOT, :]
    center = shape_sums - jnp.mean(shape_sums, axis=-1, keepdims=True)
    pooled = center * lax.rsqrt(jnp.mean(center * center, axis=-1, keepdims=True) + 1e-05)
    across = unit.shape[1] // channels
    lanes = lax.broadcasted_iota(jnp.int32, (1, unit.shape[1] - channels), 1)
    places = jnp.zeros(lanes.shape, F32)
    for i in range(owned):
        place = positive[i]
        padded = lax.div(place, owned) * SLOT + lax.rem(place, owned)
        places = places + jnp.where(lanes == i * blks + where, padded.astype(F32), 0.0)
    first = jnp.concatenate([pooled[i : i + 1, :] for i in range(across)], axis=1)
    second = jnp.concatenate([pooled[across : across + 1, :], places], axis=1)
    block = jnp.concatenate([unit, first, second], axis=0)
    pair = jnp.concatenate([block, block], axis=0).astype(BF16)
    for j in range(0, blks * SLOT, 2 * SLOT):
        out[j : j + 2 * SLOT, :] = pair


def pool(positive, sums, captions, blks, packs):
    owned, width = captions.shape
    smem = pl.BlockSpec(memory_space=pltpu.SMEM)
    vmem = pl.BlockSpec(memory_space=pltpu.VMEM)

    def body(*refs):
        pool_kernel(owned, blks, packs, *refs)

    return pl.pallas_call(
        body,
        out_shape=jax.ShapeDtypeStruct((blks * SLOT, width), BF16),
        in_specs=[smem, vmem, vmem],
        out_specs=vmem,
        compiler_params=pltpu.CompilerParams(vmem_limit_bytes=8 * 1024 * 1024),
        name="pool",
    )(positive, sums, captions)


def loss_kernel(owned, dps, blks, scale, bias, group_rows, projection, caption_grad, rows_grad):
    where = lax.axis_index("blk")
    group = blks * SLOT
    channels, width = projection.shape
    given = group_rows[...]
    wanted = lax.broadcasted_iota(jnp.int32, (2 * blks, group), 0)
    wanted = lax.rem(wanted, blks) * SLOT + owned + lax.div(wanted, blks)
    lanes = lax.broadcasted_iota(jnp.int32, (2 * blks, group), 1)
    picked = jnp.dot(
        jnp.where(wanted == lanes, 1.0, 0.0).astype(BF16), given, preferred_element_type=F32
    )
    across = width // channels
    pooled = jnp.concatenate(
        [picked[0:blks, i * channels : (i + 1) * channels] for i in range(across)]
        + [picked[blks : 2 * blks, 0:channels]],
        axis=0,
    ).astype(BF16)
    positive = jnp.sum(
        picked[blks : 2 * blks, channels : channels + owned * blks], axis=0, keepdims=True
    ).astype(jnp.int32)
    raw_embed = jnp.dot(pooled, projection[...], preferred_element_type=F32)
    norms = jnp.sqrt(jnp.sum(raw_embed * raw_embed, axis=-1, keepdims=True) + 1e-06)
    unit_shape = raw_embed / norms
    shape_embed = unit_shape.astype(BF16)
    logits = (
        scale[0] * lax.dot_general(given, shape_embed, DOT1, preferred_element_type=F32)
        + bias[0]
    )
    rows = lax.broadcasted_iota(jnp.int32, logits.shape, 0)
    label = jnp.where(rows == positive, 1.0, -1.0)
    coef = -label * jax.nn.sigmoid(-label * logits)
    coef = jnp.where(lax.rem(rows, SLOT) < owned, coef, 0.0).astype(BF16)
    mine = lax.broadcasted_iota(jnp.int32, (SLOT, group), 0) + where * SLOT
    pick = jnp.where(mine == lax.broadcasted_iota(jnp.int32, (SLOT, group), 1), 1.0, 0.0).astype(BF16)
    own_coef = jnp.dot(pick, coef, preferred_element_type=F32).astype(BF16)
    own_grad = scale[0] * jnp.dot(own_coef, shape_embed, preferred_element_type=F32)
    caption_grad[...] = own_grad[0:owned, :]
    shape_grad = scale[0] * lax.dot_general(coef, given, DOT0, preferred_element_type=F32)
    raw_grad = (shape_grad - unit_shape * jnp.sum(unit_shape * shape_grad, axis=-1, keepdims=True)) / norms
    each = channels // dps // blks
    kept = lax.broadcasted_iota(jnp.int32, (channels // blks, channels), 0)
    chosen = lax.div(kept, each) * (channels // dps) + lax.rem(kept, each) + where * each
    select = jnp.where(
        chosen == lax.broadcasted_iota(jnp.int32, (channels // blks, channels), 1), 1.0, 0.0
    ).astype(BF16)
    factors = lax.dot_general(select, pooled, DOT1, preferred_element_type=F32).astype(BF16)
    high = raw_grad.astype(BF16)
    low = (raw_grad - high.astype(F32)).astype(BF16)
    rows = jnp.dot(factors, high, preferred_element_type=F32) + jnp.dot(
        factors, low, preferred_element_type=F32
    )
    rows_grad[...] = rows.reshape(rows_grad.shape)


def loss_grads(scale, bias, group_rows, projection, owned, dps, blks):
    channels, width = projection.shape
    vmem = pl.BlockSpec(memory_space=pltpu.VMEM)
    smem = pl.BlockSpec(memory_space=pltpu.SMEM)

    def body(*refs):
        loss_kernel(owned, dps, blks, *refs)

    return pl.pallas_call(
        body,
        out_shape=(
            jax.ShapeDtypeStruct((owned, width), F32),
            jax.ShapeDtypeStruct((dps, channels // dps // blks, width), F32),
        ),
        in_specs=[smem, smem, vmem, vmem],
        out_specs=(vmem, vmem),
        compiler_params=pltpu.CompilerParams(vmem_limit_bytes=32 * 1024 * 1024),
        name="loss_grads",
    )(scale, bias, group_rows, projection)


def spread_row(parts, copies):
    sources, each, width = parts.shape
    half = width // 2

    def body(arrived, out):
        total = arrived[0]
        for d in range(1, sources):
            total = total + arrived[d]
        halves = jnp.concatenate([total[:, 0:half], total[:, half:width]], axis=0)
        out[...] = jnp.broadcast_to(halves.astype(BF16)[None], out.shape)

    vmem = pl.BlockSpec(memory_space=pltpu.VMEM)
    return pl.pallas_call(
        body,
        out_shape=jax.ShapeDtypeStruct((copies, 2 * each, half), BF16),
        in_specs=[vmem],
        out_specs=vmem,
        compiler_params=pltpu.CompilerParams(vmem_limit_bytes=8 * 1024 * 1024),
        name="spread_row",
    )(parts)


def sum_packs(every, packs):
    places, twice, half = every.shape
    each = twice // 2

    def body(parts, out):
        for b in range(places // packs):
            total = parts[b * packs].astype(F32)
            for p in range(1, packs):
                total = total + parts[b * packs + p].astype(F32)
            out[b * each : (b + 1) * each, 0:half] = total[0:each, :]
            out[b * each : (b + 1) * each, half : 2 * half] = total[each:twice, :]

    vmem = pl.BlockSpec(memory_space=pltpu.VMEM)
    return pl.pallas_call(
        body,
        out_shape=jax.ShapeDtypeStruct((places // packs * each, 2 * half), F32),
        in_specs=[vmem],
        out_specs=vmem,
        compiler_params=pltpu.CompilerParams(vmem_limit_bytes=8 * 1024 * 1024),
        name="sum_packs",
    )(every)


def exchange(array, axes, size):
    blocks = array.reshape(size, array.shape[0] // size, array.shape[1])
    return lax.all_to_all(blocks, axes, 0, 0, tiled=True).reshape(array.shape)


def shards(
    points,
    neighbours,
    tile_points,
    tile_shape,
    captions,
    positive,
    self_weight,
    neighbour_weight,
    projection,
    logit_scale,
    logit_bias,
):
    owned = captions.shape[0]
    packs = lax.axis_size("pack")
    blks = lax.axis_size("blk")
    dps = lax.axis_size("dp")
    sums = encode(
        logit_scale,
        logit_bias,
        tile_points,
        tile_shape,
        points,
        neighbours,
        self_weight,
        neighbour_weight,
        packs,
        owned,
    )
    sums = exchange(sums, "pack", packs)
    group_rows = exchange(pool(positive, sums, captions, blks, packs), "blk", blks)
    caption_grad, rows_grad = loss_grads(
        logit_scale,
        logit_bias,
        group_rows,
        projection,
        owned,
        dps,
        blks,
    )
    rows_grad = lax.all_to_all(rows_grad, "dp", 0, 0, tiled=True)
    row = spread_row(rows_grad, blks * packs)
    every = lax.all_to_all(row, ("blk", "pack"), 0, 0, tiled=True)
    projection_grad = sum_packs(every, packs)
    return (caption_grad, projection_grad)


def solution(mesh):
    in_specs = (
        P(("dp", "blk", "pack"), None),
        P(None, ("dp", "blk", "pack")),
        P(("dp", "blk", "pack")),
        P(("dp", "blk", "pack")),
        P(("dp", "blk", "pack"), None),
        P(("dp", "blk", "pack")),
        P(),
        P(),
        P(),
        P(),
        P(),
    )
    out_specs = (P(("dp", "blk", "pack"), None), P("dp", None))
    return jax.shard_map(shards, mesh=mesh, in_specs=in_specs, out_specs=out_specs, check_vma=False)
```

```python
import jax
import jax.numpy as jnp
from jax import lax
from jax.experimental import pallas as pl
from jax.experimental.pallas import tpu as pltpu
from jax.sharding import PartitionSpec as P

NEIGH = 27
TILE_PTS = 128
SLOT = 8
ENCODE_VMEM = 60 * 1024 * 1024
F32 = jnp.float32
BF16 = jnp.bfloat16
DOT0 = (((0,), (0,)), ((), ()))
DOT1 = (((1,), (1,)), ((), ()))


def encode_kernel(
    owned,
    counts_far,
    shapes_far,
    points_far,
    links_far,
    self_far,
    neighbour_far,
    sums,
    counts,
    shapes,
    points,
    links,
    self_weight,
    neighbour_weight,
    arrived,
):
    copies = [
        pltpu.make_async_copy(far, near, arrived.at[i])
        for i, (far, near) in enumerate(
            (
                (links_far, links),
                (points_far, points),
                (self_far, self_weight),
                (neighbour_far, neighbour_weight),
                (counts_far, counts),
                (shapes_far, shapes),
            )
        )
    ]
    for copy in copies:
        copy.start()
    sums[...] = jnp.zeros_like(sums)
    tiles = points.shape[0] // TILE_PTS
    rows = lax.broadcasted_iota(jnp.int32, (TILE_PTS, TILE_PTS), 0).astype(F32).astype(BF16)
    ones = jnp.ones((TILE_PTS, TILE_PTS), BF16)
    zeros = jnp.zeros((TILE_PTS, TILE_PTS), BF16)
    copies[0].wait()
    adjacencies = []
    for tile in range(tiles):
        columns = links[:, tile * TILE_PTS : (tile + 1) * TILE_PTS].astype(F32)
        adjacency = zeros
        for k in range(NEIGH):
            link = jnp.broadcast_to(columns[k : k + 1, :], (16, TILE_PTS)).astype(BF16)
            link = jnp.concatenate([link] * (TILE_PTS // 16), axis=0)
            adjacency = adjacency + jnp.where(link == rows, ones, zeros)
        adjacencies.append(adjacency)
    for copy in copies[1:]:
        copy.wait()
    aggregates = []
    for tile in range(tiles):
        span = slice(tile * TILE_PTS, (tile + 1) * TILE_PTS)
        total = lax.dot_general(adjacencies[tile], points[span, :], DOT0, preferred_element_type=F32)
        aggregates.append((total * (1.0 / NEIGH)).astype(BF16))
    features = points[...]
    before = jnp.dot(features, self_weight[...], preferred_element_type=F32) + jnp.dot(
        jnp.concatenate(aggregates, axis=0), neighbour_weight[...], preferred_element_type=F32
    )
    center = before - jnp.mean(before, axis=-1, keepdims=True)
    spread = jnp.mean(center * center, axis=-1, keepdims=True)
    hidden = features.astype(F32) + jnp.maximum(center * lax.rsqrt(spread + 1e-05), 0.0)
    point = lax.broadcasted_iota(jnp.int32, (TILE_PTS, 1), 0)
    for tile in range(tiles):
        span = slice(tile * TILE_PTS, (tile + 1) * TILE_PTS)
        kept = jnp.where(point < counts[tile], hidden[span, :], 0.0)
        place = lax.rem(shapes[tile], sums.shape[0] // SLOT * owned)
        slot = pl.ds(lax.div(place, owned) * SLOT + lax.rem(place, owned), 1)
        sums[slot, :] = sums[slot, :] + jnp.sum(kept, axis=0, keepdims=True)


def encode(counts, shapes, points, links, self_weight, neighbour_weight, packs, owned):
    channels = points.shape[1]
    vmem = pl.BlockSpec(memory_space=pltpu.VMEM)
    far = pl.BlockSpec(memory_space=pl.ANY)

    def body(*refs):
        encode_kernel(owned, *refs)

    return pl.pallas_call(
        body,
        out_shape=jax.ShapeDtypeStruct((packs * SLOT, channels), F32),
        in_specs=[far] * 6,
        out_specs=vmem,
        scratch_shapes=[
            pltpu.SMEM(counts.shape, counts.dtype),
            pltpu.SMEM(shapes.shape, shapes.dtype),
            pltpu.VMEM(points.shape, points.dtype),
            pltpu.VMEM(links.shape, links.dtype),
            pltpu.VMEM(self_weight.shape, self_weight.dtype),
            pltpu.VMEM(neighbour_weight.shape, neighbour_weight.dtype),
            pltpu.SemaphoreType.DMA((6,)),
        ],
        compiler_params=pltpu.CompilerParams(vmem_limit_bytes=ENCODE_VMEM),
        name="encode",
    )(counts, shapes, points, links, self_weight, neighbour_weight)


def pool_kernel(owned, blks, packs, scale, bias, positive, sums, captions, out):
    where = lax.axis_index("blk")
    channels = sums.shape[1]
    wide = captions[...].astype(F32)
    unit = wide / jnp.sqrt(jnp.sum(wide * wide, axis=-1, keepdims=True) + 1e-06)
    shape_sums = sums[0:SLOT, :]
    for p in range(1, packs):
        shape_sums = shape_sums + sums[p * SLOT : (p + 1) * SLOT, :]
    center = shape_sums - jnp.mean(shape_sums, axis=-1, keepdims=True)
    pooled = center * lax.rsqrt(jnp.mean(center * center, axis=-1, keepdims=True) + 1e-05)
    across = unit.shape[1] // channels
    lanes = lax.broadcasted_iota(jnp.int32, (1, unit.shape[1] - channels), 1)
    places = jnp.zeros(lanes.shape, F32)
    for i in range(owned):
        place = positive[i]
        padded = lax.div(place, owned) * SLOT + lax.rem(place, owned)
        places = places + jnp.where(lanes == i * blks + where, padded.astype(F32), 0.0)
    first = jnp.concatenate([pooled[i : i + 1, :] for i in range(across)], axis=1)
    second = jnp.concatenate([pooled[across : across + 1, :], places], axis=1)
    block = jnp.concatenate([unit, first, second], axis=0)
    pair = jnp.concatenate([block, block], axis=0).astype(BF16)
    for j in range(0, blks * SLOT, 2 * SLOT):
        out[j : j + 2 * SLOT, :] = pair


def pool(scale, bias, positive, sums, captions, blks, packs):
    owned, width = captions.shape
    smem = pl.BlockSpec(memory_space=pltpu.SMEM)
    vmem = pl.BlockSpec(memory_space=pltpu.VMEM)

    def body(*refs):
        pool_kernel(owned, blks, packs, *refs)

    return pl.pallas_call(
        body,
        out_shape=jax.ShapeDtypeStruct((blks * SLOT, width), BF16),
        in_specs=[smem, smem, smem, vmem, vmem],
        out_specs=vmem,
        compiler_params=pltpu.CompilerParams(vmem_limit_bytes=8 * 1024 * 1024),
        name="pool",
    )(scale, bias, positive, sums, captions)


def loss_kernel(owned, dps, blks, scale, bias, group_rows, projection, caption_grad, rows_grad):
    where = lax.axis_index("blk")
    group = blks * SLOT
    channels, width = projection.shape
    given = group_rows[...]
    wanted = lax.broadcasted_iota(jnp.int32, (2 * blks, group), 0)
    wanted = lax.rem(wanted, blks) * SLOT + owned + lax.div(wanted, blks)
    lanes = lax.broadcasted_iota(jnp.int32, (2 * blks, group), 1)
    picked = jnp.dot(
        jnp.where(wanted == lanes, 1.0, 0.0).astype(BF16), given, preferred_element_type=F32
    )
    across = width // channels
    pooled = jnp.concatenate(
        [picked[0:blks, i * channels : (i + 1) * channels] for i in range(across)]
        + [picked[blks : 2 * blks, 0:channels]],
        axis=0,
    ).astype(BF16)
    positive = jnp.sum(
        picked[blks : 2 * blks, channels : channels + owned * blks], axis=0, keepdims=True
    ).astype(jnp.int32)
    raw_embed = jnp.dot(pooled, projection[...], preferred_element_type=F32)
    norms = jnp.sqrt(jnp.sum(raw_embed * raw_embed, axis=-1, keepdims=True) + 1e-06)
    unit_shape = raw_embed / norms
    shape_embed = unit_shape.astype(BF16)
    logits = (
        scale[0] * lax.dot_general(given, shape_embed, DOT1, preferred_element_type=F32)
        + bias[0]
    )
    rows = lax.broadcasted_iota(jnp.int32, logits.shape, 0)
    label = jnp.where(rows == positive, 1.0, -1.0)
    coef = -label * jax.nn.sigmoid(-label * logits)
    coef = jnp.where(lax.rem(rows, SLOT) < owned, coef, 0.0).astype(BF16)
    mine = lax.broadcasted_iota(jnp.int32, (SLOT, group), 0) + where * SLOT
    pick = jnp.where(mine == lax.broadcasted_iota(jnp.int32, (SLOT, group), 1), 1.0, 0.0).astype(BF16)
    own_coef = jnp.dot(pick, coef, preferred_element_type=F32).astype(BF16)
    own_grad = scale[0] * jnp.dot(own_coef, shape_embed, preferred_element_type=F32)
    caption_grad[...] = own_grad
    shape_grad = scale[0] * lax.dot_general(coef, given, DOT0, preferred_element_type=F32)
    raw_grad = (shape_grad - unit_shape * jnp.sum(unit_shape * shape_grad, axis=-1, keepdims=True)) / norms
    each = channels // dps // blks
    kept = lax.broadcasted_iota(jnp.int32, (channels // blks, channels), 0)
    chosen = lax.div(kept, each) * (channels // dps) + lax.rem(kept, each) + where * each
    select = jnp.where(
        chosen == lax.broadcasted_iota(jnp.int32, (channels // blks, channels), 1), 1.0, 0.0
    ).astype(BF16)
    factors = lax.dot_general(select, pooled, DOT1, preferred_element_type=F32).astype(BF16)
    high = raw_grad.astype(BF16)
    low = (raw_grad - high.astype(F32)).astype(BF16)
    rows = jnp.dot(factors, high, preferred_element_type=F32) + jnp.dot(
        factors, low, preferred_element_type=F32
    )
    rows_grad[...] = rows.reshape(rows_grad.shape)


def loss_grads(scale, bias, group_rows, projection, owned, dps, blks):
    channels, width = projection.shape
    vmem = pl.BlockSpec(memory_space=pltpu.VMEM)
    smem = pl.BlockSpec(memory_space=pltpu.SMEM)

    def body(*refs):
        loss_kernel(owned, dps, blks, *refs)

    return pl.pallas_call(
        body,
        out_shape=(
            jax.ShapeDtypeStruct((SLOT, width), F32),
            jax.ShapeDtypeStruct((dps, channels // dps // blks, width), F32),
        ),
        in_specs=[smem, smem, vmem, vmem],
        out_specs=(vmem, vmem),
        compiler_params=pltpu.CompilerParams(vmem_limit_bytes=32 * 1024 * 1024),
        name="loss_grads",
    )(scale, bias, group_rows, projection)


def spread_row(parts, copies):
    sources, each, width = parts.shape
    half = width // 2

    def body(arrived, out):
        total = arrived[0]
        for d in range(1, sources):
            total = total + arrived[d]
        halves = jnp.concatenate([total[:, 0:half], total[:, half:width]], axis=0)
        out[...] = jnp.broadcast_to(halves.astype(BF16)[None], out.shape)

    vmem = pl.BlockSpec(memory_space=pltpu.VMEM)
    return pl.pallas_call(
        body,
        out_shape=jax.ShapeDtypeStruct((copies, 2 * each, half), BF16),
        in_specs=[vmem],
        out_specs=vmem,
        compiler_params=pltpu.CompilerParams(vmem_limit_bytes=8 * 1024 * 1024),
        name="spread_row",
    )(parts)


def finish(every, caption_grad, packs, owned):
    places, twice, half = every.shape
    each = twice // 2

    def body(parts, grad, out, grad_out):
        grad_out[...] = grad[0:owned, :]
        for b in range(places // packs):
            total = parts[b * packs].astype(F32)
            for p in range(1, packs):
                total = total + parts[b * packs + p].astype(F32)
            out[b * each : (b + 1) * each, 0:half] = total[0:each, :]
            out[b * each : (b + 1) * each, half : 2 * half] = total[each:twice, :]

    vmem = pl.BlockSpec(memory_space=pltpu.VMEM)
    return pl.pallas_call(
        body,
        out_shape=(
            jax.ShapeDtypeStruct((places // packs * each, 2 * half), F32),
            jax.ShapeDtypeStruct((owned, 2 * half), F32),
        ),
        in_specs=[vmem, vmem],
        out_specs=(vmem, vmem),
        compiler_params=pltpu.CompilerParams(vmem_limit_bytes=8 * 1024 * 1024),
        name="finish",
    )(every, caption_grad)


def exchange(array, axes, size):
    blocks = array.reshape(size, array.shape[0] // size, array.shape[1])
    return lax.all_to_all(blocks, axes, 0, 0, tiled=True).reshape(array.shape)


def shards(
    points,
    neighbours,
    tile_points,
    tile_shape,
    captions,
    positive,
    self_weight,
    neighbour_weight,
    projection,
    logit_scale,
    logit_bias,
):
    owned = captions.shape[0]
    packs = lax.axis_size("pack")
    blks = lax.axis_size("blk")
    dps = lax.axis_size("dp")
    sums = encode(
        tile_points,
        tile_shape,
        points,
        neighbours,
        self_weight,
        neighbour_weight,
        packs,
        owned,
    )
    sums = exchange(sums, "pack", packs)
    group_rows = exchange(pool(logit_scale, logit_bias, positive, sums, captions, blks, packs), "blk", blks)
    caption_grad, rows_grad = loss_grads(
        logit_scale,
        logit_bias,
        group_rows,
        projection,
        owned,
        dps,
        blks,
    )
    rows_grad = lax.all_to_all(rows_grad, "dp", 0, 0, tiled=True)
    row = spread_row(rows_grad, blks * packs)
    every = lax.all_to_all(row, ("blk", "pack"), 0, 0, tiled=True)
    projection_grad, caption_grad = finish(every, caption_grad, packs, owned)
    return (caption_grad, projection_grad)


def solution(mesh):
    in_specs = (
        P(("dp", "blk", "pack"), None),
        P(None, ("dp", "blk", "pack")),
        P(("dp", "blk", "pack")),
        P(("dp", "blk", "pack")),
        P(("dp", "blk", "pack"), None),
        P(("dp", "blk", "pack")),
        P(),
        P(),
        P(),
        P(),
        P(),
    )
    out_specs = (P(("dp", "blk", "pack"), None), P("dp", None))
    return jax.shard_map(shards, mesh=mesh, in_specs=in_specs, out_specs=out_specs, check_vma=False)
```

```python
import jax
import jax.numpy as jnp
from jax import lax
from jax.experimental import pallas as pl
from jax.experimental.pallas import tpu as pltpu
from jax.sharding import PartitionSpec as P

NEIGH = 27
TILE_PTS = 128
SLOT = 8
ENCODE_VMEM = 60 * 1024 * 1024
F32 = jnp.float32
BF16 = jnp.bfloat16
DOT0 = (((0,), (0,)), ((), ()))
DOT1 = (((1,), (1,)), ((), ()))


def encode_kernel(
    owned,
    counts_far,
    shapes_far,
    points_far,
    links_far,
    self_far,
    neighbour_far,
    sums,
    counts,
    shapes,
    points,
    links,
    self_weight,
    neighbour_weight,
    arrived,
):
    copies = [
        pltpu.make_async_copy(far, near, arrived.at[i])
        for i, (far, near) in enumerate(
            (
                (links_far, links),
                (points_far, points),
                (self_far, self_weight),
                (neighbour_far, neighbour_weight),
                (counts_far, counts),
                (shapes_far, shapes),
            )
        )
    ]
    for copy in copies:
        copy.start()
    sums[...] = jnp.zeros_like(sums)
    tiles = points.shape[0] // TILE_PTS
    rows = lax.broadcasted_iota(jnp.int32, (TILE_PTS, TILE_PTS), 0).astype(F32).astype(BF16)
    ones = jnp.ones((TILE_PTS, TILE_PTS), BF16)
    zeros = jnp.zeros((TILE_PTS, TILE_PTS), BF16)
    copies[0].wait()
    adjacencies = []
    for tile in range(tiles):
        columns = links[:, tile * TILE_PTS : (tile + 1) * TILE_PTS].astype(F32)
        adjacency = zeros
        for k in range(NEIGH):
            link = jnp.broadcast_to(columns[k : k + 1, :], (16, TILE_PTS)).astype(BF16)
            link = jnp.concatenate([link] * (TILE_PTS // 16), axis=0)
            adjacency = adjacency + jnp.where(link == rows, ones, zeros)
        adjacencies.append(adjacency)
    for copy in copies[1:]:
        copy.wait()
    aggregates = []
    for tile in range(tiles):
        span = slice(tile * TILE_PTS, (tile + 1) * TILE_PTS)
        total = lax.dot_general(adjacencies[tile], points[span, :], DOT0, preferred_element_type=F32)
        aggregates.append((total * (1.0 / NEIGH)).astype(BF16))
    features = points[...]
    before = jnp.dot(features, self_weight[...], preferred_element_type=F32) + jnp.dot(
        jnp.concatenate(aggregates, axis=0), neighbour_weight[...], preferred_element_type=F32
    )
    center = before - jnp.mean(before, axis=-1, keepdims=True)
    spread = jnp.mean(center * center, axis=-1, keepdims=True)
    hidden = features.astype(F32) + jnp.maximum(center * lax.rsqrt(spread + 1e-05), 0.0)
    point = lax.broadcasted_iota(jnp.int32, (TILE_PTS, 1), 0)
    for tile in range(tiles):
        span = slice(tile * TILE_PTS, (tile + 1) * TILE_PTS)
        kept = jnp.where(point < counts[tile], hidden[span, :], 0.0)
        place = lax.rem(shapes[tile], sums.shape[0] // SLOT * owned)
        slot = pl.ds(lax.div(place, owned) * SLOT + lax.rem(place, owned), 1)
        sums[slot, :] = sums[slot, :] + jnp.sum(kept, axis=0, keepdims=True)


def encode(counts, shapes, points, links, self_weight, neighbour_weight, packs, owned):
    channels = points.shape[1]
    vmem = pl.BlockSpec(memory_space=pltpu.VMEM)
    far = pl.BlockSpec(memory_space=pl.ANY)

    def body(*refs):
        encode_kernel(owned, *refs)

    return pl.pallas_call(
        body,
        out_shape=jax.ShapeDtypeStruct((packs * SLOT, channels), F32),
        in_specs=[far] * 6,
        out_specs=vmem,
        scratch_shapes=[
            pltpu.SMEM(counts.shape, counts.dtype),
            pltpu.SMEM(shapes.shape, shapes.dtype),
            pltpu.VMEM(points.shape, points.dtype),
            pltpu.VMEM(links.shape, links.dtype),
            pltpu.VMEM(self_weight.shape, self_weight.dtype),
            pltpu.VMEM(neighbour_weight.shape, neighbour_weight.dtype),
            pltpu.SemaphoreType.DMA((6,)),
        ],
        compiler_params=pltpu.CompilerParams(vmem_limit_bytes=ENCODE_VMEM),
        name="encode",
    )(counts, shapes, points, links, self_weight, neighbour_weight)


def pool_kernel(owned, blks, packs, scale, bias, positive, sums, captions, projection, out):
    channels, width = projection.shape
    wide = captions[...].astype(F32)
    unit = wide / jnp.sqrt(jnp.sum(wide * wide, axis=-1, keepdims=True) + 1e-06)
    unit = jnp.concatenate([unit, jnp.zeros((SLOT - owned, width), F32)], axis=0).astype(BF16)
    mixed = lax.dot_general(unit, projection[...], DOT1, preferred_element_type=F32)
    level = jnp.mean(mixed, axis=-1, keepdims=True)
    mixed = mixed - level
    unit = unit.astype(F32)
    shape_sums = sums[0:SLOT, :]
    for p in range(1, packs):
        shape_sums = shape_sums + sums[p * SLOT : (p + 1) * SLOT, :]
    center = shape_sums - jnp.mean(shape_sums, axis=-1, keepdims=True)
    pooled = center * lax.rsqrt(jnp.mean(center * center, axis=-1, keepdims=True) + 1e-05)
    half = width // 2
    spare = half - (owned // 2 - 1) * channels
    lanes = lax.broadcasted_iota(jnp.int32, (1, spare), 1)
    where = lax.axis_index("blk")
    places = jnp.zeros(lanes.shape, F32)
    levels = jnp.zeros(lanes.shape, F32)
    for i in range(owned):
        place = positive[i]
        padded = lax.div(place, owned) * SLOT + lax.rem(place, owned)
        places = places + jnp.where(lanes == i, padded.astype(F32), 0.0)
        levels = levels + jnp.where(lanes == where * SLOT + i, level[i : i + 1, :], 0.0)
    across = owned // 2
    first = jnp.concatenate([pooled[i : i + 1, :] for i in range(across)] + [places], axis=1)
    second = jnp.concatenate([pooled[i : i + 1, :] for i in range(across, owned)] + [levels], axis=1)
    blocks = []
    for side in range(2):
        part = unit[0:owned, side * half : (side + 1) * half]
        blocks.append(jnp.concatenate([part, mixed[0:owned, :]], axis=1))
        blocks.append(first)
        blocks.append(second)
    pair = jnp.concatenate(blocks, axis=0).astype(BF16)
    for j in range(0, blks * SLOT, 2 * SLOT):
        out[j : j + 2 * SLOT, :] = pair


def pool(scale, bias, positive, sums, captions, projection, blks, packs):
    owned, width = captions.shape
    channels = projection.shape[0]
    smem = pl.BlockSpec(memory_space=pltpu.SMEM)
    vmem = pl.BlockSpec(memory_space=pltpu.VMEM)

    def body(*refs):
        pool_kernel(owned, blks, packs, *refs)

    return pl.pallas_call(
        body,
        out_shape=jax.ShapeDtypeStruct((blks * SLOT, width // 2 + channels), BF16),
        in_specs=[smem, smem, smem, vmem, vmem, vmem],
        out_specs=vmem,
        compiler_params=pltpu.CompilerParams(vmem_limit_bytes=16 * 1024 * 1024),
        name="pool",
    )(scale, bias, positive, sums, captions, projection)


def loss_kernel(owned, dps, blks, scale, bias, group_rows, projection, caption_grad, rows_grad):
    where = lax.axis_index("blk")
    group = blks * SLOT
    channels, width = projection.shape
    half = width // 2
    across = owned // 2
    given = group_rows[...]
    wanted = lax.broadcasted_iota(jnp.int32, (2 * blks, group), 0)
    wanted = lax.rem(wanted, blks) * SLOT + owned + lax.div(wanted, blks)
    lanes = lax.broadcasted_iota(jnp.int32, (2 * blks, group), 1)
    picked = jnp.dot(
        jnp.where(wanted == lanes, 1.0, 0.0).astype(BF16), given, preferred_element_type=F32
    )
    pooled = jnp.concatenate(
        [
            picked[side * blks : (side + 1) * blks, i * channels : (i + 1) * channels]
            for side in range(2)
            for i in range(across)
        ],
        axis=0,
    ).astype(BF16)
    places = across * channels
    positive = jnp.concatenate(
        [picked[0:blks, places + i : places + i + 1] for i in range(owned)], axis=0
    ).astype(jnp.int32)
    raw_embed = jnp.dot(pooled, projection[...], preferred_element_type=F32)
    norms = jnp.sqrt(jnp.sum(raw_embed * raw_embed, axis=-1, keepdims=True) + 1e-06)
    unit_shape = raw_embed / norms
    shape_embed = unit_shape.astype(BF16)
    dots = lax.dot_general(pooled, given[:, half : half + channels], DOT1, preferred_element_type=F32)
    levels = jnp.sum(picked[blks : 2 * blks, places : places + group], axis=0, keepdims=True)
    dots = (dots + levels * jnp.sum(pooled.astype(F32), axis=-1, keepdims=True)) / norms
    logits = scale[0] * dots + bias[0]
    columns = lax.broadcasted_iota(jnp.int32, logits.shape, 1)
    label = jnp.where(columns == positive, 1.0, -1.0)
    coef = -label * jax.nn.sigmoid(-label * logits)
    coef = jnp.where(lax.rem(columns, SLOT) < owned, coef, 0.0).astype(BF16)
    mine = lax.broadcasted_iota(jnp.int32, (SLOT, group), 0) + where * SLOT
    pick = jnp.where(mine == lax.broadcasted_iota(jnp.int32, (SLOT, group), 1), 1.0, 0.0).astype(BF16)
    own_coef = lax.dot_general(pick, coef, DOT1, preferred_element_type=F32).astype(BF16)
    caption_grad[...] = scale[0] * jnp.dot(own_coef, shape_embed, preferred_element_type=F32)
    shape_grad = scale[0] * jnp.dot(coef, given[:, 0:half], preferred_element_type=F32)
    along = scale[0] * jnp.sum(coef.astype(F32) * dots, axis=-1, keepdims=True)
    side = lax.rem(where, 2)
    unit_half = jnp.where(side == 0, unit_shape[:, 0:half], unit_shape[:, half:width])
    raw_grad = (shape_grad - unit_half * along) / norms
    each = rows_grad.shape[1]
    kept = lax.broadcasted_iota(jnp.int32, (dps * each, channels), 0)
    chosen = lax.div(kept, each) * (channels // dps) + lax.rem(kept, each) + lax.div(where, 2) * each
    select = jnp.where(
        chosen == lax.broadcasted_iota(jnp.int32, (dps * each, channels), 1), 1.0, 0.0
    ).astype(BF16)
    factors = lax.dot_general(select, pooled, DOT1, preferred_element_type=F32).astype(BF16)
    high = raw_grad.astype(BF16)
    low = (raw_grad - high.astype(F32)).astype(BF16)
    rows = jnp.dot(factors, high, preferred_element_type=F32) + jnp.dot(
        factors, low, preferred_element_type=F32
    )
    rows_grad[...] = rows.reshape(rows_grad.shape)


def loss_grads(scale, bias, group_rows, projection, owned, dps, blks):
    channels, width = projection.shape
    smem = pl.BlockSpec(memory_space=pltpu.SMEM)
    vmem = pl.BlockSpec(memory_space=pltpu.VMEM)

    def body(*refs):
        loss_kernel(owned, dps, blks, *refs)

    return pl.pallas_call(
        body,
        out_shape=(
            jax.ShapeDtypeStruct((SLOT, width), F32),
            jax.ShapeDtypeStruct((dps, 2 * channels // dps // blks, width // 2), F32),
        ),
        in_specs=[smem, smem, vmem, vmem],
        out_specs=(vmem, vmem),
        compiler_params=pltpu.CompilerParams(vmem_limit_bytes=32 * 1024 * 1024),
        name="loss_grads",
    )(scale, bias, group_rows, projection)


def spread_row(parts, copies):
    sources, each, half = parts.shape

    def body(arrived, out):
        total = arrived[0]
        for d in range(1, sources):
            total = total + arrived[d]
        out[...] = jnp.broadcast_to(total.astype(BF16)[None], out.shape)

    vmem = pl.BlockSpec(memory_space=pltpu.VMEM)
    return pl.pallas_call(
        body,
        out_shape=jax.ShapeDtypeStruct((copies, each, half), BF16),
        in_specs=[vmem],
        out_specs=vmem,
        compiler_params=pltpu.CompilerParams(vmem_limit_bytes=8 * 1024 * 1024),
        name="spread_row",
    )(parts)


def finish(every, caption_grad, packs, owned):
    places, each, half = every.shape

    def body(parts, grad, out, grad_out):
        grad_out[...] = grad[0:owned, :]
        for b in range(places // packs):
            total = parts[b * packs].astype(F32)
            for p in range(1, packs):
                total = total + parts[b * packs + p].astype(F32)
            row, side = b // 2, b % 2
            out[row * each : (row + 1) * each, side * half : (side + 1) * half] = total

    vmem = pl.BlockSpec(memory_space=pltpu.VMEM)
    return pl.pallas_call(
        body,
        out_shape=(
            jax.ShapeDtypeStruct((places // packs // 2 * each, 2 * half), F32),
            jax.ShapeDtypeStruct((owned, 2 * half), F32),
        ),
        in_specs=[vmem, vmem],
        out_specs=(vmem, vmem),
        compiler_params=pltpu.CompilerParams(vmem_limit_bytes=8 * 1024 * 1024),
        name="finish",
    )(every, caption_grad)


def exchange(array, axes, size):
    blocks = array.reshape(size, array.shape[0] // size, array.shape[1])
    return lax.all_to_all(blocks, axes, 0, 0, tiled=True).reshape(array.shape)


def shards(
    points,
    neighbours,
    tile_points,
    tile_shape,
    captions,
    positive,
    self_weight,
    neighbour_weight,
    projection,
    logit_scale,
    logit_bias,
):
    owned = captions.shape[0]
    packs = lax.axis_size("pack")
    blks = lax.axis_size("blk")
    dps = lax.axis_size("dp")
    sums = encode(
        tile_points,
        tile_shape,
        points,
        neighbours,
        self_weight,
        neighbour_weight,
        packs,
        owned,
    )
    sums = exchange(sums, "pack", packs)
    group_rows = exchange(pool(logit_scale, logit_bias, positive, sums, captions, projection, blks, packs), "blk", blks)
    caption_grad, rows_grad = loss_grads(
        logit_scale,
        logit_bias,
        group_rows,
        projection,
        owned,
        dps,
        blks,
    )
    rows_grad = lax.all_to_all(rows_grad, "dp", 0, 0, tiled=True)
    row = spread_row(rows_grad, blks * packs)
    every = lax.all_to_all(row, ("blk", "pack"), 0, 0, tiled=True)
    projection_grad, caption_grad = finish(every, caption_grad, packs, owned)
    return (caption_grad, projection_grad)


def solution(mesh):
    in_specs = (
        P(("dp", "blk", "pack"), None),
        P(None, ("dp", "blk", "pack")),
        P(("dp", "blk", "pack")),
        P(("dp", "blk", "pack")),
        P(("dp", "blk", "pack"), None),
        P(("dp", "blk", "pack")),
        P(),
        P(),
        P(),
        P(),
        P(),
    )
    out_specs = (P(("dp", "blk", "pack"), None), P("dp", None))
    return jax.shard_map(shards, mesh=mesh, in_specs=in_specs, out_specs=out_specs, check_vma=False)
```

```python
import jax
import jax.numpy as jnp
from jax import lax
from jax.experimental import pallas as pl
from jax.experimental.pallas import tpu as pltpu
from jax.sharding import PartitionSpec as P

NEIGH = 27
TILE_PTS = 128
SLOT = 8
ENCODE_VMEM = 60 * 1024 * 1024
F32 = jnp.float32
BF16 = jnp.bfloat16
DOT0 = (((0,), (0,)), ((), ()))
DOT1 = (((1,), (1,)), ((), ()))


def encode_kernel(
    owned,
    counts_far,
    shapes_far,
    points_far,
    links_far,
    self_far,
    neighbour_far,
    sums,
    counts,
    shapes,
    points,
    links,
    self_weight,
    neighbour_weight,
    arrived,
):
    copies = [
        pltpu.make_async_copy(far, near, arrived.at[i])
        for i, (far, near) in enumerate(
            (
                (links_far, links),
                (points_far, points),
                (self_far, self_weight),
                (neighbour_far, neighbour_weight),
                (counts_far, counts),
                (shapes_far, shapes),
            )
        )
    ]
    for copy in copies:
        copy.start()
    sums[...] = jnp.zeros_like(sums)
    tiles = points.shape[0] // TILE_PTS
    rows = lax.broadcasted_iota(jnp.int32, (TILE_PTS, TILE_PTS), 0).astype(F32).astype(BF16)
    ones = jnp.ones((TILE_PTS, TILE_PTS), BF16)
    zeros = jnp.zeros((TILE_PTS, TILE_PTS), BF16)
    copies[0].wait()
    adjacencies = []
    for tile in range(tiles):
        columns = links[:, tile * TILE_PTS : (tile + 1) * TILE_PTS].astype(F32)
        adjacency = zeros
        for k in range(NEIGH):
            link = jnp.broadcast_to(columns[k : k + 1, :], (16, TILE_PTS)).astype(BF16)
            link = jnp.concatenate([link] * (TILE_PTS // 16), axis=0)
            adjacency = adjacency + jnp.where(link == rows, ones, zeros)
        adjacencies.append(adjacency)
    for copy in copies[1:]:
        copy.wait()
    aggregates = []
    for tile in range(tiles):
        span = slice(tile * TILE_PTS, (tile + 1) * TILE_PTS)
        total = lax.dot_general(adjacencies[tile], points[span, :], DOT0, preferred_element_type=F32)
        aggregates.append((total * (1.0 / NEIGH)).astype(BF16))
    features = points[...]
    before = jnp.dot(features, self_weight[...], preferred_element_type=F32) + jnp.dot(
        jnp.concatenate(aggregates, axis=0), neighbour_weight[...], preferred_element_type=F32
    )
    center = before - jnp.mean(before, axis=-1, keepdims=True)
    spread = jnp.mean(center * center, axis=-1, keepdims=True)
    hidden = features.astype(F32) + jnp.maximum(center * lax.rsqrt(spread + 1e-05), 0.0)
    point = lax.broadcasted_iota(jnp.int32, (TILE_PTS, 1), 0)
    for tile in range(tiles):
        span = slice(tile * TILE_PTS, (tile + 1) * TILE_PTS)
        kept = jnp.where(point < counts[tile], hidden[span, :], 0.0)
        place = lax.rem(shapes[tile], sums.shape[0] // SLOT * owned)
        slot = pl.ds(lax.div(place, owned) * SLOT + lax.rem(place, owned), 1)
        sums[slot, :] = sums[slot, :] + jnp.sum(kept, axis=0, keepdims=True)


def encode(counts, shapes, points, links, self_weight, neighbour_weight, packs, owned):
    channels = points.shape[1]
    vmem = pl.BlockSpec(memory_space=pltpu.VMEM)
    far = pl.BlockSpec(memory_space=pl.ANY)

    def body(*refs):
        encode_kernel(owned, *refs)

    return pl.pallas_call(
        body,
        out_shape=jax.ShapeDtypeStruct((packs * SLOT, channels), F32),
        in_specs=[far] * 6,
        out_specs=vmem,
        scratch_shapes=[
            pltpu.SMEM(counts.shape, counts.dtype),
            pltpu.SMEM(shapes.shape, shapes.dtype),
            pltpu.VMEM(points.shape, points.dtype),
            pltpu.VMEM(links.shape, links.dtype),
            pltpu.VMEM(self_weight.shape, self_weight.dtype),
            pltpu.VMEM(neighbour_weight.shape, neighbour_weight.dtype),
            pltpu.SemaphoreType.DMA((6,)),
        ],
        compiler_params=pltpu.CompilerParams(vmem_limit_bytes=ENCODE_VMEM),
        name="encode",
    )(counts, shapes, points, links, self_weight, neighbour_weight)


def caption_kernel(owned, blks, positive, encoded, captions, projection, out):
    channels, width = projection.shape
    half = width // 2
    wide = captions[...].astype(F32)
    unit = wide / jnp.sqrt(jnp.sum(wide * wide, axis=-1, keepdims=True) + 1e-06)
    unit = jnp.concatenate([unit, jnp.zeros((SLOT - owned, width), F32)], axis=0).astype(BF16)
    mixed = lax.dot_general(unit, projection[...], DOT1, preferred_element_type=F32)
    level = jnp.mean(mixed, axis=-1, keepdims=True)
    mixed = mixed - level
    unit = unit.astype(F32)
    where = lax.axis_index("blk")
    lanes = lax.broadcasted_iota(jnp.int32, (1, out.shape[1]), 1) - owned // 2 * channels
    places = jnp.zeros(lanes.shape, F32)
    levels = jnp.zeros(lanes.shape, F32)
    for i in range(owned):
        place = positive[i]
        padded = lax.div(place, owned) * SLOT + lax.rem(place, owned)
        places = places + jnp.where(lanes == i, padded.astype(F32), 0.0)
        levels = levels + jnp.where(lanes == where * SLOT + i, level[i : i + 1, :], 0.0)
    for side in range(2):
        part = unit[0:owned, side * half : (side + 1) * half]
        rows = [jnp.concatenate([part, mixed[0:owned, :]], axis=1), places, levels]
        out[side * SLOT : (side + 1) * SLOT, :] = jnp.concatenate(rows, axis=0)


def caption_rows(positive, encoded, captions, projection, blks):
    owned, width = captions.shape
    channels = projection.shape[0]
    smem = pl.BlockSpec(memory_space=pltpu.SMEM)
    vmem = pl.BlockSpec(memory_space=pltpu.VMEM)

    def body(*refs):
        caption_kernel(owned, blks, *refs)

    return pl.pallas_call(
        body,
        out_shape=jax.ShapeDtypeStruct((2 * SLOT, width // 2 + channels), F32),
        in_specs=[smem, pl.BlockSpec(memory_space=pl.ANY), vmem, vmem],
        out_specs=vmem,
        compiler_params=pltpu.CompilerParams(vmem_limit_bytes=16 * 1024 * 1024),
        name="caption_rows",
    )(positive, encoded, captions, projection)


def pool_kernel(owned, blks, packs, scale, bias, sums, rows, out):
    channels = sums.shape[1]
    shape_sums = sums[0:SLOT, :]
    for p in range(1, packs):
        shape_sums = shape_sums + sums[p * SLOT : (p + 1) * SLOT, :]
    center = shape_sums - jnp.mean(shape_sums, axis=-1, keepdims=True)
    pooled = center * lax.rsqrt(jnp.mean(center * center, axis=-1, keepdims=True) + 1e-05)
    across = owned // 2
    spare = across * channels
    blocks = []
    for side in range(2):
        top = side * SLOT
        blocks.append(rows[top : top + owned, :])
        for line in range(2):
            held = [pooled[i : i + 1, :] for i in range(line * across, (line + 1) * across)]
            row = top + owned + line
            blocks.append(jnp.concatenate(held + [rows[row : row + 1, spare:]], axis=1))
    pair = jnp.concatenate(blocks, axis=0).astype(BF16)
    for j in range(0, blks * SLOT, 2 * SLOT):
        out[j : j + 2 * SLOT, :] = pair


def pool(scale, bias, sums, rows, owned, blks, packs):
    smem = pl.BlockSpec(memory_space=pltpu.SMEM)
    vmem = pl.BlockSpec(memory_space=pltpu.VMEM)

    def body(*refs):
        pool_kernel(owned, blks, packs, *refs)

    return pl.pallas_call(
        body,
        out_shape=jax.ShapeDtypeStruct((blks * SLOT, rows.shape[1]), BF16),
        in_specs=[smem, smem, vmem, vmem],
        out_specs=vmem,
        compiler_params=pltpu.CompilerParams(vmem_limit_bytes=16 * 1024 * 1024),
        name="pool",
    )(scale, bias, sums, rows)


def loss_kernel(owned, dps, blks, scale, bias, group_rows, projection, caption_grad, rows_grad):
    where = lax.axis_index("blk")
    group = blks * SLOT
    channels, width = projection.shape
    half = width // 2
    across = owned // 2
    given = group_rows[...]
    wanted = lax.broadcasted_iota(jnp.int32, (2 * blks, group), 0)
    wanted = lax.rem(wanted, blks) * SLOT + owned + lax.div(wanted, blks)
    lanes = lax.broadcasted_iota(jnp.int32, (2 * blks, group), 1)
    picked = jnp.dot(
        jnp.where(wanted == lanes, 1.0, 0.0).astype(BF16), given, preferred_element_type=F32
    )
    pooled = jnp.concatenate(
        [
            picked[side * blks : (side + 1) * blks, i * channels : (i + 1) * channels]
            for side in range(2)
            for i in range(across)
        ],
        axis=0,
    ).astype(BF16)
    places = across * channels
    positive = jnp.concatenate(
        [picked[0:blks, places + i : places + i + 1] for i in range(owned)], axis=0
    ).astype(jnp.int32)
    raw_embed = jnp.dot(pooled, projection[...], preferred_element_type=F32)
    norms = jnp.sqrt(jnp.sum(raw_embed * raw_embed, axis=-1, keepdims=True) + 1e-06)
    unit_shape = raw_embed / norms
    shape_embed = unit_shape.astype(BF16)
    dots = lax.dot_general(pooled, given[:, half : half + channels], DOT1, preferred_element_type=F32)
    levels = jnp.sum(picked[blks : 2 * blks, places : places + group], axis=0, keepdims=True)
    dots = (dots + levels * jnp.sum(pooled.astype(F32), axis=-1, keepdims=True)) / norms
    logits = scale[0] * dots + bias[0]
    columns = lax.broadcasted_iota(jnp.int32, logits.shape, 1)
    label = jnp.where(columns == positive, 1.0, -1.0)
    coef = -label * jax.nn.sigmoid(-label * logits)
    coef = jnp.where(lax.rem(columns, SLOT) < owned, coef, 0.0).astype(BF16)
    mine = lax.broadcasted_iota(jnp.int32, (SLOT, group), 0) + where * SLOT
    pick = jnp.where(mine == lax.broadcasted_iota(jnp.int32, (SLOT, group), 1), 1.0, 0.0).astype(BF16)
    own_coef = lax.dot_general(pick, coef, DOT1, preferred_element_type=F32).astype(BF16)
    caption_grad[...] = scale[0] * jnp.dot(own_coef, shape_embed, preferred_element_type=F32)
    shape_grad = scale[0] * jnp.dot(coef, given[:, 0:half], preferred_element_type=F32)
    along = scale[0] * jnp.sum(coef.astype(F32) * dots, axis=-1, keepdims=True)
    side = lax.rem(where, 2)
    unit_half = jnp.where(side == 0, unit_shape[:, 0:half], unit_shape[:, half:width])
    raw_grad = (shape_grad - unit_half * along) / norms
    each = rows_grad.shape[1]
    kept = lax.broadcasted_iota(jnp.int32, (dps * each, channels), 0)
    chosen = lax.div(kept, each) * (channels // dps) + lax.rem(kept, each) + lax.div(where, 2) * each
    select = jnp.where(
        chosen == lax.broadcasted_iota(jnp.int32, (dps * each, channels), 1), 1.0, 0.0
    ).astype(BF16)
    factors = lax.dot_general(select, pooled, DOT1, preferred_element_type=F32).astype(BF16)
    high = raw_grad.astype(BF16)
    low = (raw_grad - high.astype(F32)).astype(BF16)
    rows = jnp.dot(factors, high, preferred_element_type=F32) + jnp.dot(
        factors, low, preferred_element_type=F32
    )
    rows_grad[...] = rows.reshape(rows_grad.shape)


def loss_grads(scale, bias, group_rows, projection, owned, dps, blks):
    channels, width = projection.shape
    smem = pl.BlockSpec(memory_space=pltpu.SMEM)
    vmem = pl.BlockSpec(memory_space=pltpu.VMEM)

    def body(*refs):
        loss_kernel(owned, dps, blks, *refs)

    return pl.pallas_call(
        body,
        out_shape=(
            jax.ShapeDtypeStruct((SLOT, width), F32),
            jax.ShapeDtypeStruct((dps, 2 * channels // dps // blks, width // 2), F32),
        ),
        in_specs=[smem, smem, vmem, vmem],
        out_specs=(vmem, vmem),
        compiler_params=pltpu.CompilerParams(vmem_limit_bytes=32 * 1024 * 1024),
        name="loss_grads",
    )(scale, bias, group_rows, projection)


def spread_row(parts, copies):
    sources, each, half = parts.shape

    def body(arrived, out):
        total = arrived[0]
        for d in range(1, sources):
            total = total + arrived[d]
        out[...] = jnp.broadcast_to(total.astype(BF16)[None], out.shape)

    vmem = pl.BlockSpec(memory_space=pltpu.VMEM)
    return pl.pallas_call(
        body,
        out_shape=jax.ShapeDtypeStruct((copies, each, half), BF16),
        in_specs=[vmem],
        out_specs=vmem,
        compiler_params=pltpu.CompilerParams(vmem_limit_bytes=8 * 1024 * 1024),
        name="spread_row",
    )(parts)


def finish(every, caption_grad, packs, owned):
    places, each, half = every.shape

    def body(parts, grad, out, grad_out):
        grad_out[...] = grad[0:owned, :]
        for b in range(places // packs):
            total = parts[b * packs].astype(F32)
            for p in range(1, packs):
                total = total + parts[b * packs + p].astype(F32)
            row, side = b // 2, b % 2
            out[row * each : (row + 1) * each, side * half : (side + 1) * half] = total

    vmem = pl.BlockSpec(memory_space=pltpu.VMEM)
    return pl.pallas_call(
        body,
        out_shape=(
            jax.ShapeDtypeStruct((places // packs // 2 * each, 2 * half), F32),
            jax.ShapeDtypeStruct((owned, 2 * half), F32),
        ),
        in_specs=[vmem, vmem],
        out_specs=(vmem, vmem),
        compiler_params=pltpu.CompilerParams(vmem_limit_bytes=8 * 1024 * 1024),
        name="finish",
    )(every, caption_grad)


def exchange(array, axes, size):
    blocks = array.reshape(size, array.shape[0] // size, array.shape[1])
    return lax.all_to_all(blocks, axes, 0, 0, tiled=True).reshape(array.shape)


def shards(
    points,
    neighbours,
    tile_points,
    tile_shape,
    captions,
    positive,
    self_weight,
    neighbour_weight,
    projection,
    logit_scale,
    logit_bias,
):
    owned = captions.shape[0]
    packs = lax.axis_size("pack")
    blks = lax.axis_size("blk")
    dps = lax.axis_size("dp")
    sums = encode(
        tile_points,
        tile_shape,
        points,
        neighbours,
        self_weight,
        neighbour_weight,
        packs,
        owned,
    )
    rows = caption_rows(positive, sums, captions, projection, blks)
    sums = exchange(sums, "pack", packs)
    group_rows = exchange(pool(logit_scale, logit_bias, sums, rows, owned, blks, packs), "blk", blks)
    caption_grad, rows_grad = loss_grads(
        logit_scale,
        logit_bias,
        group_rows,
        projection,
        owned,
        dps,
        blks,
    )
    rows_grad = lax.all_to_all(rows_grad, "dp", 0, 0, tiled=True)
    row = spread_row(rows_grad, blks * packs)
    every = lax.all_to_all(row, ("blk", "pack"), 0, 0, tiled=True)
    projection_grad, caption_grad = finish(every, caption_grad, packs, owned)
    return (caption_grad, projection_grad)


def solution(mesh):
    in_specs = (
        P(("dp", "blk", "pack"), None),
        P(None, ("dp", "blk", "pack")),
        P(("dp", "blk", "pack")),
        P(("dp", "blk", "pack")),
        P(("dp", "blk", "pack"), None),
        P(("dp", "blk", "pack")),
        P(),
        P(),
        P(),
        P(),
        P(),
    )
    out_specs = (P(("dp", "blk", "pack"), None), P("dp", None))
    return jax.shard_map(shards, mesh=mesh, in_specs=in_specs, out_specs=out_specs, check_vma=False)
```

```python
import jax
import jax.numpy as jnp
from jax import lax
from jax.experimental import pallas as pl
from jax.experimental.pallas import tpu as pltpu
from jax.sharding import PartitionSpec as P

NEIGH = 27
TILE_PTS = 128
SLOT = 8
ENCODE_VMEM = 60 * 1024 * 1024
F32 = jnp.float32
BF16 = jnp.bfloat16
DOT0 = (((0,), (0,)), ((), ()))
DOT1 = (((1,), (1,)), ((), ()))


def encode_kernel(
    owned,
    counts_far,
    shapes_far,
    points_far,
    links_far,
    self_far,
    neighbour_far,
    sums,
    counts,
    shapes,
    points,
    links,
    self_weight,
    neighbour_weight,
    arrived,
):
    copies = [
        pltpu.make_async_copy(far, near, arrived.at[i])
        for i, (far, near) in enumerate(
            (
                (links_far, links),
                (points_far, points),
                (self_far, self_weight),
                (neighbour_far, neighbour_weight),
                (counts_far, counts),
                (shapes_far, shapes),
            )
        )
    ]
    for copy in copies:
        copy.start()
    sums[...] = jnp.zeros_like(sums)
    tiles = points.shape[0] // TILE_PTS
    rows = lax.broadcasted_iota(jnp.int32, (TILE_PTS, TILE_PTS), 0).astype(F32).astype(BF16)
    ones = jnp.ones((TILE_PTS, TILE_PTS), BF16)
    zeros = jnp.zeros((TILE_PTS, TILE_PTS), BF16)
    copies[0].wait()
    adjacencies = []
    for tile in range(tiles):
        columns = links[:, tile * TILE_PTS : (tile + 1) * TILE_PTS].astype(F32)
        adjacency = zeros
        for k in range(NEIGH):
            link = jnp.broadcast_to(columns[k : k + 1, :], (16, TILE_PTS)).astype(BF16)
            link = jnp.concatenate([link] * (TILE_PTS // 16), axis=0)
            adjacency = adjacency + jnp.where(link == rows, ones, zeros)
        adjacencies.append(adjacency)
    for copy in copies[1:]:
        copy.wait()
    aggregates = []
    for tile in range(tiles):
        span = slice(tile * TILE_PTS, (tile + 1) * TILE_PTS)
        total = lax.dot_general(adjacencies[tile], points[span, :], DOT0, preferred_element_type=F32)
        aggregates.append((total * (1.0 / NEIGH)).astype(BF16))
    features = points[...]
    before = jnp.dot(features, self_weight[...], preferred_element_type=F32) + jnp.dot(
        jnp.concatenate(aggregates, axis=0), neighbour_weight[...], preferred_element_type=F32
    )
    center = before - jnp.mean(before, axis=-1, keepdims=True)
    spread = jnp.mean(center * center, axis=-1, keepdims=True)
    hidden = features.astype(F32) + jnp.maximum(center * lax.rsqrt(spread + 1e-05), 0.0)
    point = lax.broadcasted_iota(jnp.int32, (TILE_PTS, 1), 0)
    for tile in range(tiles):
        span = slice(tile * TILE_PTS, (tile + 1) * TILE_PTS)
        kept = jnp.where(point < counts[tile], hidden[span, :], 0.0)
        place = lax.rem(shapes[tile], sums.shape[0] // SLOT * owned)
        slot = pl.ds(lax.div(place, owned) * SLOT + lax.rem(place, owned), 1)
        sums[slot, :] = sums[slot, :] + jnp.sum(kept, axis=0, keepdims=True)


def encode(counts, shapes, points, links, self_weight, neighbour_weight, packs, owned):
    channels = points.shape[1]
    vmem = pl.BlockSpec(memory_space=pltpu.VMEM)
    far = pl.BlockSpec(memory_space=pl.ANY)

    def body(*refs):
        encode_kernel(owned, *refs)

    return pl.pallas_call(
        body,
        out_shape=jax.ShapeDtypeStruct((packs * SLOT, channels), F32),
        in_specs=[far] * 6,
        out_specs=vmem,
        scratch_shapes=[
            pltpu.SMEM(counts.shape, counts.dtype),
            pltpu.SMEM(shapes.shape, shapes.dtype),
            pltpu.VMEM(points.shape, points.dtype),
            pltpu.VMEM(links.shape, links.dtype),
            pltpu.VMEM(self_weight.shape, self_weight.dtype),
            pltpu.VMEM(neighbour_weight.shape, neighbour_weight.dtype),
            pltpu.SemaphoreType.DMA((6,)),
        ],
        compiler_params=pltpu.CompilerParams(vmem_limit_bytes=ENCODE_VMEM),
        name="encode",
    )(counts, shapes, points, links, self_weight, neighbour_weight)


def caption_kernel(owned, blks, positive, encoded, captions, projection, out):
    channels, width = projection.shape
    half = width // 2
    wide = captions[...].astype(F32)
    unit = wide / jnp.sqrt(jnp.sum(wide * wide, axis=-1, keepdims=True) + 1e-06)
    unit = jnp.concatenate([unit, jnp.zeros((SLOT - owned, width), F32)], axis=0).astype(BF16)
    mixed = lax.dot_general(unit, projection[...], DOT1, preferred_element_type=F32)
    level = jnp.mean(mixed, axis=-1, keepdims=True)
    mixed = mixed - level
    unit = unit.astype(F32)
    where = lax.axis_index("blk")
    lanes = lax.broadcasted_iota(jnp.int32, (1, out.shape[1]), 1) - owned // 2 * channels
    places = jnp.zeros(lanes.shape, F32)
    levels = jnp.zeros(lanes.shape, F32)
    for i in range(owned):
        place = positive[i]
        padded = lax.div(place, owned) * SLOT + lax.rem(place, owned)
        places = places + jnp.where(lanes == i, padded.astype(F32), 0.0)
        levels = levels + jnp.where(lanes == where * SLOT + i, level[i : i + 1, :], 0.0)
    for side in range(2):
        part = unit[0:owned, side * half : (side + 1) * half]
        rows = [jnp.concatenate([part, mixed[0:owned, :]], axis=1), places, levels]
        out[side * SLOT : (side + 1) * SLOT, :] = jnp.concatenate(rows, axis=0)


def caption_rows(positive, encoded, captions, projection, blks):
    owned, width = captions.shape
    channels = projection.shape[0]
    smem = pl.BlockSpec(memory_space=pltpu.SMEM)
    vmem = pl.BlockSpec(memory_space=pltpu.VMEM)

    def body(*refs):
        caption_kernel(owned, blks, *refs)

    return pl.pallas_call(
        body,
        out_shape=jax.ShapeDtypeStruct((2 * SLOT, width // 2 + channels), F32),
        in_specs=[smem, pl.BlockSpec(memory_space=pl.ANY), vmem, vmem],
        out_specs=vmem,
        compiler_params=pltpu.CompilerParams(vmem_limit_bytes=16 * 1024 * 1024),
        name="caption_rows",
    )(positive, encoded, captions, projection)


def pool_kernel(owned, blks, packs, scale, bias, sums, rows, out):
    channels = sums.shape[1]
    shape_sums = sums[0:SLOT, :]
    for p in range(1, packs):
        shape_sums = shape_sums + sums[p * SLOT : (p + 1) * SLOT, :]
    center = shape_sums - jnp.mean(shape_sums, axis=-1, keepdims=True)
    pooled = center * lax.rsqrt(jnp.mean(center * center, axis=-1, keepdims=True) + 1e-05)
    across = owned // 2
    spare = across * channels
    blocks = []
    for side in range(2):
        top = side * SLOT
        blocks.append(rows[top : top + owned, :])
        for line in range(2):
            held = [pooled[i : i + 1, :] for i in range(line * across, (line + 1) * across)]
            row = top + owned + line
            blocks.append(jnp.concatenate(held + [rows[row : row + 1, spare:]], axis=1))
    pair = jnp.concatenate(blocks, axis=0).astype(BF16)
    for j in range(0, blks * SLOT, 2 * SLOT):
        out[j : j + 2 * SLOT, :] = pair


def pool(scale, bias, sums, rows, owned, blks, packs):
    smem = pl.BlockSpec(memory_space=pltpu.SMEM)
    vmem = pl.BlockSpec(memory_space=pltpu.VMEM)

    def body(*refs):
        pool_kernel(owned, blks, packs, *refs)

    return pl.pallas_call(
        body,
        out_shape=jax.ShapeDtypeStruct((blks * SLOT, rows.shape[1]), BF16),
        in_specs=[smem, smem, vmem, vmem],
        out_specs=vmem,
        compiler_params=pltpu.CompilerParams(vmem_limit_bytes=16 * 1024 * 1024),
        name="pool",
    )(scale, bias, sums, rows)


def loss_kernel(owned, dps, blks, scale, bias, group_rows, projection, caption_grad, rows_grad):
    where = lax.axis_index("blk")
    group = blks * SLOT
    channels, width = projection.shape
    half = width // 2
    across = owned // 2
    given = group_rows[...]
    wanted = lax.broadcasted_iota(jnp.int32, (2 * blks, group), 0)
    wanted = lax.rem(wanted, blks) * SLOT + owned + lax.div(wanted, blks)
    lanes = lax.broadcasted_iota(jnp.int32, (2 * blks, group), 1)
    picked = jnp.dot(
        jnp.where(wanted == lanes, 1.0, 0.0).astype(BF16), given, preferred_element_type=F32
    )
    pooled = jnp.concatenate(
        [
            picked[side * blks : (side + 1) * blks, i * channels : (i + 1) * channels]
            for side in range(2)
            for i in range(across)
        ],
        axis=0,
    ).astype(BF16)
    places = across * channels
    positive = jnp.concatenate(
        [picked[0:blks, places + i : places + i + 1] for i in range(owned)], axis=0
    ).astype(jnp.int32)
    raw_embed = jnp.dot(pooled, projection[...], preferred_element_type=F32)
    norms = jnp.sqrt(jnp.sum(raw_embed * raw_embed, axis=-1, keepdims=True) + 1e-06)
    unit_shape = raw_embed / norms
    shape_embed = unit_shape.astype(BF16)
    dots = lax.dot_general(pooled, given[:, half : half + channels], DOT1, preferred_element_type=F32)
    levels = jnp.sum(picked[blks : 2 * blks, places : places + group], axis=0, keepdims=True)
    dots = (dots + levels * jnp.sum(pooled.astype(F32), axis=-1, keepdims=True)) / norms
    logits = scale[0] * dots + bias[0]
    columns = lax.broadcasted_iota(jnp.int32, logits.shape, 1)
    label = jnp.where(columns == positive, 1.0, -1.0)
    coef = -label * jax.nn.sigmoid(-label * logits)
    coef = jnp.where(lax.rem(columns, SLOT) < owned, coef, 0.0).astype(BF16)
    mine = lax.broadcasted_iota(jnp.int32, (SLOT, group), 0) + where * SLOT
    pick = jnp.where(mine == lax.broadcasted_iota(jnp.int32, (SLOT, group), 1), 1.0, 0.0).astype(BF16)
    own_coef = lax.dot_general(pick, coef, DOT1, preferred_element_type=F32).astype(BF16)
    caption_grad[...] = scale[0] * jnp.dot(own_coef, shape_embed, preferred_element_type=F32)
    shape_grad = scale[0] * jnp.dot(coef, given[:, 0:half], preferred_element_type=F32)
    along = scale[0] * jnp.sum(coef.astype(F32) * dots, axis=-1, keepdims=True)
    side = lax.rem(where, 2)
    unit_half = jnp.where(side == 0, unit_shape[:, 0:half], unit_shape[:, half:width])
    raw_grad = (shape_grad - unit_half * along) / norms
    each = rows_grad.shape[1]
    kept = lax.broadcasted_iota(jnp.int32, (dps * each, channels), 0)
    chosen = lax.div(kept, each) * (channels // dps) + lax.rem(kept, each) + lax.div(where, 2) * each
    select = jnp.where(
        chosen == lax.broadcasted_iota(jnp.int32, (dps * each, channels), 1), 1.0, 0.0
    ).astype(BF16)
    factors = lax.dot_general(select, pooled, DOT1, preferred_element_type=F32).astype(BF16)
    high = raw_grad.astype(BF16)
    low = (raw_grad - high.astype(F32)).astype(BF16)
    rows = jnp.dot(factors, high, preferred_element_type=F32) + jnp.dot(
        factors, low, preferred_element_type=F32
    )
    rows_grad[...] = rows.reshape(rows_grad.shape).astype(BF16)


def loss_grads(scale, bias, group_rows, projection, owned, dps, blks):
    channels, width = projection.shape
    smem = pl.BlockSpec(memory_space=pltpu.SMEM)
    vmem = pl.BlockSpec(memory_space=pltpu.VMEM)

    def body(*refs):
        loss_kernel(owned, dps, blks, *refs)

    return pl.pallas_call(
        body,
        out_shape=(
            jax.ShapeDtypeStruct((SLOT, width), F32),
            jax.ShapeDtypeStruct((dps, 2 * channels // dps // blks, width // 2), BF16),
        ),
        in_specs=[smem, smem, vmem, vmem],
        out_specs=(vmem, vmem),
        compiler_params=pltpu.CompilerParams(vmem_limit_bytes=32 * 1024 * 1024),
        name="loss_grads",
    )(scale, bias, group_rows, projection)


def spread_row(parts, copies):
    sources, each, half = parts.shape

    def body(arrived, out):
        total = arrived[0].astype(F32)
        for d in range(1, sources):
            total = total + arrived[d].astype(F32)
        out[...] = jnp.broadcast_to(total.astype(BF16)[None], out.shape)

    vmem = pl.BlockSpec(memory_space=pltpu.VMEM)
    return pl.pallas_call(
        body,
        out_shape=jax.ShapeDtypeStruct((copies, each, half), BF16),
        in_specs=[vmem],
        out_specs=vmem,
        compiler_params=pltpu.CompilerParams(vmem_limit_bytes=8 * 1024 * 1024),
        name="spread_row",
    )(parts)


def finish(every, caption_grad, packs, owned):
    places, each, half = every.shape

    def body(parts, grad, out, grad_out):
        grad_out[...] = grad[0:owned, :]
        for b in range(places // packs):
            total = parts[b * packs].astype(F32)
            for p in range(1, packs):
                total = total + parts[b * packs + p].astype(F32)
            row, side = b // 2, b % 2
            out[row * each : (row + 1) * each, side * half : (side + 1) * half] = total

    vmem = pl.BlockSpec(memory_space=pltpu.VMEM)
    return pl.pallas_call(
        body,
        out_shape=(
            jax.ShapeDtypeStruct((places // packs // 2 * each, 2 * half), F32),
            jax.ShapeDtypeStruct((owned, 2 * half), F32),
        ),
        in_specs=[vmem, vmem],
        out_specs=(vmem, vmem),
        compiler_params=pltpu.CompilerParams(vmem_limit_bytes=8 * 1024 * 1024),
        name="finish",
    )(every, caption_grad)


def exchange(array, axes, size):
    blocks = array.reshape(size, array.shape[0] // size, array.shape[1])
    return lax.all_to_all(blocks, axes, 0, 0, tiled=True).reshape(array.shape)


def shards(
    points,
    neighbours,
    tile_points,
    tile_shape,
    captions,
    positive,
    self_weight,
    neighbour_weight,
    projection,
    logit_scale,
    logit_bias,
):
    owned = captions.shape[0]
    packs = lax.axis_size("pack")
    blks = lax.axis_size("blk")
    dps = lax.axis_size("dp")
    sums = encode(
        tile_points,
        tile_shape,
        points,
        neighbours,
        self_weight,
        neighbour_weight,
        packs,
        owned,
    )
    rows = caption_rows(positive, sums, captions, projection, blks)
    sums = exchange(sums, "pack", packs)
    group_rows = exchange(pool(logit_scale, logit_bias, sums, rows, owned, blks, packs), "blk", blks)
    caption_grad, rows_grad = loss_grads(
        logit_scale,
        logit_bias,
        group_rows,
        projection,
        owned,
        dps,
        blks,
    )
    rows_grad = lax.all_to_all(rows_grad, "dp", 0, 0, tiled=True)
    row = spread_row(rows_grad, blks * packs)
    every = lax.all_to_all(row, ("blk", "pack"), 0, 0, tiled=True)
    projection_grad, caption_grad = finish(every, caption_grad, packs, owned)
    return (caption_grad, projection_grad)


def solution(mesh):
    in_specs = (
        P(("dp", "blk", "pack"), None),
        P(None, ("dp", "blk", "pack")),
        P(("dp", "blk", "pack")),
        P(("dp", "blk", "pack")),
        P(("dp", "blk", "pack"), None),
        P(("dp", "blk", "pack")),
        P(),
        P(),
        P(),
        P(),
        P(),
    )
    out_specs = (P(("dp", "blk", "pack"), None), P("dp", None))
    return jax.shard_map(shards, mesh=mesh, in_specs=in_specs, out_specs=out_specs, check_vma=False)
```

```python
import jax
import jax.numpy as jnp
from jax import lax
from jax.experimental import pallas as pl
from jax.experimental.pallas import tpu as pltpu
from jax.sharding import PartitionSpec as P

NEIGH = 27
TILE_PTS = 128
SLOT = 8
ENCODE_VMEM = 60 * 1024 * 1024
F32 = jnp.float32
BF16 = jnp.bfloat16
DOT0 = (((0,), (0,)), ((), ()))
DOT1 = (((1,), (1,)), ((), ()))


def encode_kernel(
    owned,
    counts_far,
    shapes_far,
    points_far,
    links_far,
    self_far,
    neighbour_far,
    sums,
    counts,
    shapes,
    points,
    links,
    self_weight,
    neighbour_weight,
    arrived,
):
    cut = 3 * TILE_PTS
    copies = [
        pltpu.make_async_copy(far, near, arrived.at[i])
        for i, (far, near) in enumerate(
            (
                (links_far.at[:, 0:cut], links.at[:, 0:cut]),
                (links_far.at[:, cut : links.shape[1]], links.at[:, cut : links.shape[1]]),
                (points_far, points),
                (self_far, self_weight),
                (neighbour_far, neighbour_weight),
                (counts_far, counts),
                (shapes_far, shapes),
            )
        )
    ]
    for copy in copies:
        copy.start()
    sums[...] = jnp.zeros_like(sums)
    tiles = points.shape[0] // TILE_PTS
    rows = lax.broadcasted_iota(jnp.int32, (TILE_PTS, TILE_PTS), 0).astype(F32).astype(BF16)
    ones = jnp.ones((TILE_PTS, TILE_PTS), BF16)
    zeros = jnp.zeros((TILE_PTS, TILE_PTS), BF16)
    copies[0].wait()
    adjacencies = []
    for tile in range(tiles):
        if tile * TILE_PTS == cut:
            copies[1].wait()
        columns = links[:, tile * TILE_PTS : (tile + 1) * TILE_PTS].astype(F32)
        parts = [zeros, zeros]
        for k in range(NEIGH):
            link = jnp.broadcast_to(columns[k : k + 1, :], (16, TILE_PTS)).astype(BF16)
            link = jnp.concatenate([link] * (TILE_PTS // 16), axis=0)
            one = jnp.where(link == rows, ones, zeros)
            parts[k % 2] = one if k < 2 else parts[k % 2] + one
        adjacencies.append(parts[0] + parts[1])
    for copy in copies[2:]:
        copy.wait()
    aggregates = []
    for tile in range(tiles):
        span = slice(tile * TILE_PTS, (tile + 1) * TILE_PTS)
        total = lax.dot_general(adjacencies[tile], points[span, :], DOT0, preferred_element_type=F32)
        aggregates.append((total * (1.0 / NEIGH)).astype(BF16))
    features = points[...]
    before = jnp.dot(features, self_weight[...], preferred_element_type=F32) + jnp.dot(
        jnp.concatenate(aggregates, axis=0), neighbour_weight[...], preferred_element_type=F32
    )
    center = before - jnp.mean(before, axis=-1, keepdims=True)
    spread = jnp.mean(center * center, axis=-1, keepdims=True)
    hidden = features.astype(F32) + jnp.maximum(center * lax.rsqrt(spread + 1e-05), 0.0)
    point = lax.broadcasted_iota(jnp.int32, (TILE_PTS, 1), 0)
    for tile in range(tiles):
        span = slice(tile * TILE_PTS, (tile + 1) * TILE_PTS)
        kept = jnp.where(point < counts[tile], hidden[span, :], 0.0)
        place = lax.rem(shapes[tile], sums.shape[0] // SLOT * owned)
        slot = pl.ds(lax.div(place, owned) * SLOT + lax.rem(place, owned), 1)
        sums[slot, :] = sums[slot, :] + jnp.sum(kept, axis=0, keepdims=True)


def encode(counts, shapes, points, links, self_weight, neighbour_weight, packs, owned):
    channels = points.shape[1]
    vmem = pl.BlockSpec(memory_space=pltpu.VMEM)
    far = pl.BlockSpec(memory_space=pl.ANY)

    def body(*refs):
        encode_kernel(owned, *refs)

    return pl.pallas_call(
        body,
        out_shape=jax.ShapeDtypeStruct((packs * SLOT, channels), F32),
        in_specs=[far] * 6,
        out_specs=vmem,
        scratch_shapes=[
            pltpu.SMEM(counts.shape, counts.dtype),
            pltpu.SMEM(shapes.shape, shapes.dtype),
            pltpu.VMEM(points.shape, points.dtype),
            pltpu.VMEM(links.shape, links.dtype),
            pltpu.VMEM(self_weight.shape, self_weight.dtype),
            pltpu.VMEM(neighbour_weight.shape, neighbour_weight.dtype),
            pltpu.SemaphoreType.DMA((7,)),
        ],
        compiler_params=pltpu.CompilerParams(vmem_limit_bytes=ENCODE_VMEM),
        name="encode",
    )(counts, shapes, points, links, self_weight, neighbour_weight)


def caption_kernel(owned, blks, positive, encoded, captions, projection, out):
    channels, width = projection.shape
    half = width // 2
    wide = captions[...].astype(F32)
    unit = wide / jnp.sqrt(jnp.sum(wide * wide, axis=-1, keepdims=True) + 1e-06)
    unit = jnp.concatenate([unit, jnp.zeros((SLOT - owned, width), F32)], axis=0).astype(BF16)
    mixed = lax.dot_general(unit, projection[...], DOT1, preferred_element_type=F32)
    level = jnp.mean(mixed, axis=-1, keepdims=True)
    mixed = mixed - level
    unit = unit.astype(F32)
    where = lax.axis_index("blk")
    lanes = lax.broadcasted_iota(jnp.int32, (1, out.shape[1]), 1) - owned // 2 * channels
    places = jnp.zeros(lanes.shape, F32)
    levels = jnp.zeros(lanes.shape, F32)
    for i in range(owned):
        place = positive[i]
        padded = lax.div(place, owned) * SLOT + lax.rem(place, owned)
        places = places + jnp.where(lanes == i, padded.astype(F32), 0.0)
        levels = levels + jnp.where(lanes == where * SLOT + i, level[i : i + 1, :], 0.0)
    for side in range(2):
        part = unit[0:owned, side * half : (side + 1) * half]
        rows = [jnp.concatenate([part, mixed[0:owned, :]], axis=1), places, levels]
        out[side * SLOT : (side + 1) * SLOT, :] = jnp.concatenate(rows, axis=0)


def caption_rows(positive, encoded, captions, projection, blks):
    owned, width = captions.shape
    channels = projection.shape[0]
    smem = pl.BlockSpec(memory_space=pltpu.SMEM)
    vmem = pl.BlockSpec(memory_space=pltpu.VMEM)

    def body(*refs):
        caption_kernel(owned, blks, *refs)

    return pl.pallas_call(
        body,
        out_shape=jax.ShapeDtypeStruct((2 * SLOT, width // 2 + channels), F32),
        in_specs=[smem, pl.BlockSpec(memory_space=pl.ANY), vmem, vmem],
        out_specs=vmem,
        compiler_params=pltpu.CompilerParams(vmem_limit_bytes=16 * 1024 * 1024),
        name="caption_rows",
    )(positive, encoded, captions, projection)


def pool_kernel(owned, blks, packs, scale, bias, sums, rows, out):
    channels = sums.shape[1]
    shape_sums = sums[0:SLOT, :]
    for p in range(1, packs):
        shape_sums = shape_sums + sums[p * SLOT : (p + 1) * SLOT, :]
    center = shape_sums - jnp.mean(shape_sums, axis=-1, keepdims=True)
    pooled = center * lax.rsqrt(jnp.mean(center * center, axis=-1, keepdims=True) + 1e-05)
    across = owned // 2
    spare = across * channels
    blocks = []
    for side in range(2):
        top = side * SLOT
        blocks.append(rows[top : top + owned, :])
        for line in range(2):
            held = [pooled[i : i + 1, :] for i in range(line * across, (line + 1) * across)]
            row = top + owned + line
            blocks.append(jnp.concatenate(held + [rows[row : row + 1, spare:]], axis=1))
    pair = jnp.concatenate(blocks, axis=0).astype(BF16)
    for j in range(0, blks * SLOT, 2 * SLOT):
        out[j : j + 2 * SLOT, :] = pair


def pool(scale, bias, sums, rows, owned, blks, packs):
    smem = pl.BlockSpec(memory_space=pltpu.SMEM)
    vmem = pl.BlockSpec(memory_space=pltpu.VMEM)

    def body(*refs):
        pool_kernel(owned, blks, packs, *refs)

    return pl.pallas_call(
        body,
        out_shape=jax.ShapeDtypeStruct((blks * SLOT, rows.shape[1]), BF16),
        in_specs=[smem, smem, vmem, vmem],
        out_specs=vmem,
        compiler_params=pltpu.CompilerParams(vmem_limit_bytes=16 * 1024 * 1024),
        name="pool",
    )(scale, bias, sums, rows)


def loss_kernel(owned, dps, blks, scale, bias, group_rows, projection, caption_grad, rows_grad):
    where = lax.axis_index("blk")
    group = blks * SLOT
    channels, width = projection.shape
    half = width // 2
    across = owned // 2
    given = group_rows[...]
    wanted = lax.broadcasted_iota(jnp.int32, (2 * blks, group), 0)
    wanted = lax.rem(wanted, blks) * SLOT + owned + lax.div(wanted, blks)
    lanes = lax.broadcasted_iota(jnp.int32, (2 * blks, group), 1)
    picked = jnp.dot(
        jnp.where(wanted == lanes, 1.0, 0.0).astype(BF16), given, preferred_element_type=F32
    )
    pooled = jnp.concatenate(
        [
            picked[side * blks : (side + 1) * blks, i * channels : (i + 1) * channels]
            for side in range(2)
            for i in range(across)
        ],
        axis=0,
    ).astype(BF16)
    places = across * channels
    positive = jnp.concatenate(
        [picked[0:blks, places + i : places + i + 1] for i in range(owned)], axis=0
    ).astype(jnp.int32)
    raw_embed = jnp.dot(pooled, projection[...], preferred_element_type=F32)
    norms = jnp.sqrt(jnp.sum(raw_embed * raw_embed, axis=-1, keepdims=True) + 1e-06)
    unit_shape = raw_embed / norms
    shape_embed = unit_shape.astype(BF16)
    dots = lax.dot_general(pooled, given[:, half : half + channels], DOT1, preferred_element_type=F32)
    levels = jnp.sum(picked[blks : 2 * blks, places : places + group], axis=0, keepdims=True)
    dots = (dots + levels * jnp.sum(pooled.astype(F32), axis=-1, keepdims=True)) / norms
    logits = scale[0] * dots + bias[0]
    columns = lax.broadcasted_iota(jnp.int32, logits.shape, 1)
    label = jnp.where(columns == positive, 1.0, -1.0)
    coef = -label * jax.nn.sigmoid(-label * logits)
    coef = jnp.where(lax.rem(columns, SLOT) < owned, coef, 0.0).astype(BF16)
    mine = lax.broadcasted_iota(jnp.int32, (SLOT, group), 0) + where * SLOT
    pick = jnp.where(mine == lax.broadcasted_iota(jnp.int32, (SLOT, group), 1), 1.0, 0.0).astype(BF16)
    own_coef = lax.dot_general(pick, coef, DOT1, preferred_element_type=F32).astype(BF16)
    caption_grad[...] = scale[0] * jnp.dot(own_coef, shape_embed, preferred_element_type=F32)
    shape_grad = scale[0] * jnp.dot(coef, given[:, 0:half], preferred_element_type=F32)
    along = scale[0] * jnp.sum(coef.astype(F32) * dots, axis=-1, keepdims=True)
    side = lax.rem(where, 2)
    unit_half = jnp.where(side == 0, unit_shape[:, 0:half], unit_shape[:, half:width])
    raw_grad = (shape_grad - unit_half * along) / norms
    each = rows_grad.shape[1]
    kept = lax.broadcasted_iota(jnp.int32, (dps * each, channels), 0)
    chosen = lax.div(kept, each) * (channels // dps) + lax.rem(kept, each) + lax.div(where, 2) * each
    select = jnp.where(
        chosen == lax.broadcasted_iota(jnp.int32, (dps * each, channels), 1), 1.0, 0.0
    ).astype(BF16)
    factors = lax.dot_general(select, pooled, DOT1, preferred_element_type=F32).astype(BF16)
    high = raw_grad.astype(BF16)
    low = (raw_grad - high.astype(F32)).astype(BF16)
    rows = jnp.dot(factors, high, preferred_element_type=F32) + jnp.dot(
        factors, low, preferred_element_type=F32
    )
    rows_grad[...] = rows.reshape(rows_grad.shape).astype(BF16)


def loss_grads(scale, bias, group_rows, projection, owned, dps, blks):
    channels, width = projection.shape
    smem = pl.BlockSpec(memory_space=pltpu.SMEM)
    vmem = pl.BlockSpec(memory_space=pltpu.VMEM)

    def body(*refs):
        loss_kernel(owned, dps, blks, *refs)

    return pl.pallas_call(
        body,
        out_shape=(
            jax.ShapeDtypeStruct((SLOT, width), F32),
            jax.ShapeDtypeStruct((dps, 2 * channels // dps // blks, width // 2), BF16),
        ),
        in_specs=[smem, smem, vmem, vmem],
        out_specs=(vmem, vmem),
        compiler_params=pltpu.CompilerParams(vmem_limit_bytes=32 * 1024 * 1024),
        name="loss_grads",
    )(scale, bias, group_rows, projection)


def spread_row(parts, copies):
    sources, each, half = parts.shape

    def body(arrived, out):
        total = arrived[0].astype(F32)
        for d in range(1, sources):
            total = total + arrived[d].astype(F32)
        out[...] = jnp.broadcast_to(total.astype(BF16)[None], out.shape)

    vmem = pl.BlockSpec(memory_space=pltpu.VMEM)
    return pl.pallas_call(
        body,
        out_shape=jax.ShapeDtypeStruct((copies, each, half), BF16),
        in_specs=[vmem],
        out_specs=vmem,
        compiler_params=pltpu.CompilerParams(vmem_limit_bytes=8 * 1024 * 1024),
        name="spread_row",
    )(parts)


def finish(every, caption_grad, packs, owned):
    places, each, half = every.shape

    def body(parts, grad, out, grad_out):
        grad_out[...] = grad[0:owned, :]
        for b in range(places // packs):
            total = parts[b * packs].astype(F32)
            for p in range(1, packs):
                total = total + parts[b * packs + p].astype(F32)
            row, side = b // 2, b % 2
            out[row * each : (row + 1) * each, side * half : (side + 1) * half] = total

    vmem = pl.BlockSpec(memory_space=pltpu.VMEM)
    return pl.pallas_call(
        body,
        out_shape=(
            jax.ShapeDtypeStruct((places // packs // 2 * each, 2 * half), F32),
            jax.ShapeDtypeStruct((owned, 2 * half), F32),
        ),
        in_specs=[vmem, vmem],
        out_specs=(vmem, vmem),
        compiler_params=pltpu.CompilerParams(vmem_limit_bytes=8 * 1024 * 1024),
        name="finish",
    )(every, caption_grad)


def exchange(array, axes, size):
    blocks = array.reshape(size, array.shape[0] // size, array.shape[1])
    return lax.all_to_all(blocks, axes, 0, 0, tiled=True).reshape(array.shape)


def shards(
    points,
    neighbours,
    tile_points,
    tile_shape,
    captions,
    positive,
    self_weight,
    neighbour_weight,
    projection,
    logit_scale,
    logit_bias,
):
    owned = captions.shape[0]
    packs = lax.axis_size("pack")
    blks = lax.axis_size("blk")
    dps = lax.axis_size("dp")
    sums = encode(
        tile_points,
        tile_shape,
        points,
        neighbours,
        self_weight,
        neighbour_weight,
        packs,
        owned,
    )
    rows = caption_rows(positive, sums, captions, projection, blks)
    sums = exchange(sums, "pack", packs)
    group_rows = exchange(pool(logit_scale, logit_bias, sums, rows, owned, blks, packs), "blk", blks)
    caption_grad, rows_grad = loss_grads(
        logit_scale,
        logit_bias,
        group_rows,
        projection,
        owned,
        dps,
        blks,
    )
    rows_grad = lax.all_to_all(rows_grad, "dp", 0, 0, tiled=True)
    row = spread_row(rows_grad, blks * packs)
    every = lax.all_to_all(row, ("blk", "pack"), 0, 0, tiled=True)
    projection_grad, caption_grad = finish(every, caption_grad, packs, owned)
    return (caption_grad, projection_grad)


def solution(mesh):
    in_specs = (
        P(("dp", "blk", "pack"), None),
        P(None, ("dp", "blk", "pack")),
        P(("dp", "blk", "pack")),
        P(("dp", "blk", "pack")),
        P(("dp", "blk", "pack"), None),
        P(("dp", "blk", "pack")),
        P(),
        P(),
        P(),
        P(),
        P(),
    )
    out_specs = (P(("dp", "blk", "pack"), None), P("dp", None))
    return jax.shard_map(shards, mesh=mesh, in_specs=in_specs, out_specs=out_specs, check_vma=False)
```
